512 devices in a mesh: dom: 64 (over y_lo, z, core), orb: 8 (over y_hi, x).
Axes of the slice: x: 4, y: 4 (y_hi: 2, y_lo: 2; y = y_hi * 2 + y_lo), z: 16, core: 2. Of those that a mesh axis runs over, the one named last changes fastest.
Arguments:
- orbitals: float32 [96, 64, 6, 8, 128], P('orb', 'dom'), may hold values from -6 to 6
- potential: float32 [64, 6, 8, 128], P('dom'), may hold values from 0.1 to 1.5
Outputs:
- rotated: float32 [96, 64, 6, 8, 128], P('orb', 'dom')
- subspace_h: float32 [96, 96], replicated
The draws below stay inside these ranges and needn't reach their ends.
All inputs are finite; a program needn't handle non-finite values.
Results may differ from the reference program's by a relative error of at most 0.000071.
Values sent between devices are 32-bit elements; how exact they have to be, the bound alone decides.
A program may use at most 64 MiB of HBM per device.

```python
import jax
import jax.numpy as jnp
from jax import lax

NORB = 96
DEGREE = 8
RADIUS = 6
PCOLS = 8
CX = 6
CY = 8
NZ = 128
PROWS = 8
PENCILS = 64
NX = 48
NY = 64


def levels(own_key, dims, shards, least, high):
    gain, own = 1.0, jax.random.fold_in(own_key, 6)
    for axis_at, shards_of in shards:
        heights = jnp.exp(jax.random.uniform(jax.random.fold_in(own, axis_at), (shards_of,), jnp.float32, least / len(shards), high / len(shards)))
        gain = gain * jnp.repeat(heights, dims[axis_at] // shards_of).reshape([-1 if axis == axis_at else 1 for axis in range(len(dims))])
    return gain


def centred(rng, extent, deviation, bound, shards=(), kind=jnp.bfloat16):
    entries = deviation * jax.random.normal(rng, extent, jnp.float32)
    if shards:
        entries = entries * levels(rng, extent, shards, -0.22, 0.18)
    return jnp.clip(entries, -bound, bound).astype(kind)


def setup_inputs(seed: int = 0) -> dict:
    splits = jax.random.split(jax.random.key(seed), 3)
    orbitals = centred(splits[0], (NORB, PENCILS, CX, CY, NZ), 1.0, 6.0, ((0, 8), (1, 64)), jnp.float32)
    potential = jnp.clip(0.1 + 1.4 * jax.random.uniform(splits[1], (PENCILS, CX, CY, NZ), jnp.float32) ** levels(splits[1], (PENCILS, CX, CY, NZ), ((0, 64),), -0.2, 0.2), 0.1, 1.5)
    return dict(orbitals=orbitals, potential=potential)


COEF = (-5369.0 / 1800.0, 12.0 / 7.0, -15.0 / 56.0, 10.0 / 189.0, -1.0 / 112.0, 2.0 / 1925.0, -1.0 / 16632.0)
E_HALF = 6.0
CENTER = 8.0
A_LOW = 0.0

def to_grid(block):
    count = block.shape[0]
    block = block.reshape(count, PROWS, PCOLS, CX, CY, NZ).transpose(0, 1, 3, 2, 4, 5)
    return block.reshape(count, PROWS * CX, PCOLS * CY, NZ)

def to_pencils(field):
    count = field.shape[0]
    field = field.reshape(count, PROWS, CX, PCOLS, CY, NZ).transpose(0, 1, 3, 2, 4, 5)
    return field.reshape(count, PROWS * PCOLS, CX, CY, NZ)

def hamiltonian(field, pot):
    nx, ny, nz = field.shape
    rad = RADIUS
    padded = jnp.pad(field, rad)
    lap = 3.0 * COEF[0] * field
    for k in range(1, rad + 1):
        term = padded[rad + k:rad + k + nx, rad:rad + ny, rad:rad + nz] + padded[rad - k:rad - k + nx, rad:rad + ny, rad:rad + nz]
        term = term + padded[rad:rad + nx, rad + k:rad + k + ny, rad:rad + nz] + padded[rad:rad + nx, rad - k:rad - k + ny, rad:rad + nz]
        term = term + padded[rad:rad + nx, rad:rad + ny, rad + k:rad + k + nz] + padded[rad:rad + nx, rad:rad + ny, rad - k:rad - k + nz]
        lap = lap + COEF[k] * term
    return -0.5 * lap + pot * field

def reference(orbitals, potential):
    grid = to_grid(orbitals)
    pot = to_grid(potential[None])[0]

    def filter_one(start_field):
        sigma = E_HALF / (A_LOW - CENTER)
        sigma_one = sigma
        older = start_field
        newer = (hamiltonian(older, pot) - CENTER * older) * (sigma_one / E_HALF)
        for step in range(2, DEGREE + 1):
            sigma_next = 1.0 / (2.0 / sigma_one - sigma)
            latest = (hamiltonian(newer, pot) - CENTER * newer) * (2.0 * sigma_next / E_HALF) - sigma * sigma_next * older
            older = newer
            newer = latest
            sigma = sigma_next
        return (newer, hamiltonian(newer, pot))
    filtered, applied = lax.map(filter_one, grid)
    cells = NX * NY * NZ
    flat_f = filtered.reshape(NORB, cells)
    flat_a = applied.reshape(NORB, cells)
    hi = lax.Precision.HIGHEST
    intersection = jnp.dot(flat_f, flat_f.T, precision=hi) / float(cells)
    projected = jnp.dot(flat_f, flat_a.T, precision=hi) / float(cells)
    lower = jnp.linalg.cholesky(intersection)
    inverse = lax.linalg.triangular_solve(lower, jnp.eye(NORB, dtype=jnp.float32), left_side=True, lower=True)
    subspace_h = jnp.dot(jnp.dot(inverse, projected, precision=hi), inverse.T, precision=hi)
    rotated = jnp.dot(inverse, flat_f, precision=hi).reshape(NORB, NX, NY, NZ)
    return (to_pencils(rotated), subspace_h)
```

```python
import jax
import jax.numpy as jnp
import numpy as np
from jax import lax
from jax.experimental import pallas as pl
from jax.experimental.pallas import tpu as pltpu
from jax.sharding import PartitionSpec as P

MESH = pl.DeviceIdType.MESH
HI = lax.Precision.HIGHEST

NORB = 96
DEGREE = 8
RADIUS = 6
CELLS = 48 * 64 * 128

COEF = (
    -5369.0 / 1800.0,
    12.0 / 7.0,
    -15.0 / 56.0,
    10.0 / 189.0,
    -1.0 / 112.0,
    2.0 / 1925.0,
    -1.0 / 16632.0,
)
E_HALF = 6.0
CENTER = 8.0
A_LOW = 0.0

ROWS = 24
EXT_ROWS = ROWS + 2 * RADIUS
EXT_COLS = 80


def z_weights():
    w = np.zeros((128, 128), np.float64)
    for k in range(-RADIUS, RADIUS + 1):
        w += np.diag(np.full(128 - abs(k), COEF[abs(k)]), k)
    w += 2.0 * COEF[0] * np.eye(128)
    return (-0.5 * w).astype(np.float32)


def step_scalars():
    rows = [(0.0, 0.0, 0.0)]
    sigma = sigma_one = E_HALF / (A_LOW - CENTER)
    rows.append((sigma_one / E_HALF, CENTER, 0.0))
    for _ in range(2, DEGREE + 1):
        sigma_next = 1.0 / (2.0 / sigma_one - sigma)
        rows.append((2.0 * sigma_next / E_HALF, CENTER, sigma * sigma_next))
        sigma = sigma_next
    rows.append((1.0, 0.0, 0.0))
    return np.asarray(rows, np.float32).reshape(-1)


def place():
    d, o = lax.axis_index("dom"), lax.axis_index("orb")
    y_lo, z, c = d // 32, (d // 2) % 16, d % 2
    off = jnp.maximum(z - y_lo, 0)
    slot = (off * 3 + 2) // 8
    active = (z >= y_lo) & (slot < 6) & ((slot * 8) // 3 == off)
    return d, o, y_lo, z, c, slot, active


def holder(j, c):
    y_lo, slot = j % 2, j // 2
    return y_lo * 32 + ((slot * 8) // 3 + y_lo) * 2 + c


def copy_to(src, dst, send, recv, **axes):
    return pltpu.make_async_remote_copy(
        src_ref=src, dst_ref=dst, send_sem=send, recv_sem=recv, device_id=axes, device_id_type=MESH
    )


def landed(ref, sem):
    pltpu.make_async_copy(ref, ref, sem).wait()


def loop(n, body):
    lax.fori_loop(0, n, lambda i, carry: (body(i), carry)[1], 0)


def filter_kernel(
    scal_ref, orb_ref, pot_ref, w_ref, fall_ref, gram_ref,
    buf, potb, zs, fback, aback, fall, aall,
    in_send, in_recv, p_send, p_recv, g_send, g_recv, h_send, h_recv,
    f_send, f_recv, a_send, a_recv, rf_send, rf_recv, ra_send, ra_recv,
):
    d, o, y_lo, z, c, slot, active = place()
    orbital = slot * 2 + y_lo
    prow, pcol = d // 8, d % 8
    selfpair = active & (c == y_lo)

    @pl.when(active)
    def _():
        zero = jnp.zeros((EXT_COLS, 128), jnp.float32)

        def clear(i):
            buf[0, i] = zero
            buf[1, i] = zero

        loop(EXT_ROWS, clear)

    barrier = pltpu.get_barrier_semaphore()

    def greet(cond, **axes):
        @pl.when(cond)
        def _():
            pl.semaphore_signal(barrier, inc=1, device_id=axes, device_id_type=MESH)

    def greet_holder(j):
        t = holder(j, y_lo)
        greet(t != d, dom=t)

    def greet_orb(b):
        greet(b != o, orb=b)

    def greet_source(m):
        t = c * 32 + m
        greet(t != d, dom=t)

    loop(12, greet_holder)
    loop(8, greet_orb)

    @pl.when(active)
    def _():
        loop(32, greet_source)
        pl.semaphore_signal(barrier, inc=1, device_id={"dom": d + 1 - 2 * c}, device_id_type=MESH)

    pl.semaphore_wait(barrier, 19 + 33 * active.astype(jnp.int32) - 2 * selfpair.astype(jnp.int32))

    col0 = pl.multiple_of(pcol * 8, 8)

    def pot_copy(j):
        return copy_to(
            pot_ref.at[0, o], potb.at[prow % 4, o, pl.ds(col0, 8)], p_send.at[j], p_recv, dom=holder(j, y_lo)
        )

    def send_pot(i):
        j = (i + z) % 12

        @pl.when(holder(j, y_lo) != d)
        def _():
            pot_copy(j).start()

        @pl.when(holder(j, y_lo) == d)
        def _():
            pltpu.make_async_copy(pot_ref.at[0, o], potb.at[prow % 4, o, pl.ds(col0, 8)], p_recv).start()

    @pl.when(o < 6)
    def _():
        loop(12, send_pot)

    def in_dst():
        return buf.at[0, pl.ds(RADIUS + (prow % 4) * 6, 6), pl.ds(pl.multiple_of(8 + pcol * 8, 8), 8)]

    def in_copy(j):
        return copy_to(orb_ref.at[j, 0], in_dst(), in_send.at[j], in_recv, dom=holder(j, y_lo))

    def send_in(i):
        j = (i + z) % 12

        @pl.when(holder(j, y_lo) != d)
        def _():
            in_copy(j).start()

        @pl.when(holder(j, y_lo) == d)
        def _():
            pltpu.make_async_copy(orb_ref.at[j, 0], in_dst(), in_recv).start()

    loop(12, send_in)

    def share_copy(b):
        return copy_to(potb.at[:, o], potb.at[:, o], g_send.at[b], g_recv.at[o], orb=b)

    def out_src(m, at):
        q, col = m // 8, m % 8
        return buf.at[at, pl.ds(RADIUS + q * 6, 6), pl.ds(pl.multiple_of(8 + col * 8, 8), 8)]

    def send_out(at, back, send, recv):
        def one(i):
            m = (i + d) % 32
            t = c * 32 + m

            @pl.when(t != d)
            def _():
                copy_to(out_src(m, at), back.at[orbital], send.at[m], recv, dom=t).start()

            @pl.when(t == d)
            def _():
                pltpu.make_async_copy(out_src(m, at), back.at[orbital], recv).start()

        loop(32, one)

    def sent_out(at, back, send, recv):
        def one(m):
            t = c * 32 + m

            @pl.when(t != d)
            def _():
                copy_to(out_src(m, at), back.at[orbital], send.at[m], recv, dom=t).wait_send()

        loop(32, one)

    @pl.when(active)
    def _():
        @pl.when(o < 6)
        def _():
            landed(potb.at[:, 0], p_recv)

            def share(b):
                @pl.when(b != o)
                def _():
                    share_copy(b).start()

            loop(8, share)

        def shared(r):
            @pl.when(r != o)
            def _():
                landed(potb.at[:, 0], g_recv.at[r])

        loop(6, shared)
        landed(buf.at[0, pl.ds(RADIUS, ROWS), pl.ds(8, 64)], in_recv)

        def step(s):
            cur, new = (s + 1) % 2, s % 2
            halo = copy_to(
                buf.at[cur, pl.ds(24 - 18 * c, 6), pl.ds(8, 64)],
                buf.at[cur, pl.ds(30 * c, 6), pl.ds(8, 64)],
                h_send.at[cur], h_recv.at[cur], dom=d + 1 - 2 * c,
            )
            halo.start()
            scale, shift, past = scal_ref[3 * s], scal_ref[3 * s + 1], scal_ref[3 * s + 2]

            def block(i):
                @pl.when(i == 3)
                def _():
                    halo.wait_recv()

                blk = jnp.where(c == 0, i, 3 - i)
                r0 = RADIUS + blk * 6
                x = buf[cur, pl.ds(r0, 6), 8:72, :].reshape(6 * 64, 128)
                zs[...] = jnp.dot(
                    x, w_ref[...], precision=HI, preferred_element_type=jnp.float32
                ).reshape(6, 64, 128)
                for yt in range(8):
                    y0 = 8 + 8 * yt
                    col = [buf[cur, r0 - RADIUS + m, y0 : y0 + 8, :] for m in range(18)]
                    for i6 in range(6):
                        r = r0 + i6
                        acc = zs[i6, y0 - 8 : y0, :]
                        mid = col[i6 + RADIUS]
                        for k in range(1, RADIUS + 1):
                            term = col[i6 + RADIUS + k] + col[i6 + RADIUS - k]
                            term = term + (
                                buf[cur, r, y0 + k : y0 + k + 8, :] + buf[cur, r, y0 - k : y0 - k + 8, :]
                            )
                            acc = acc + (-0.5 * COEF[k]) * term
                        acc = acc + (potb[blk, i6, y0 - 8 : y0, :] - shift) * mid
                        buf[new, r, y0 : y0 + 8, :] = scale * acc - past * buf[new, r, y0 : y0 + 8, :]

            loop(4, block)
            halo.wait_send()

            @pl.when(s == DEGREE)
            def _():
                send_out(0, fback, f_send, f_recv)

        loop(DEGREE + 1, lambda s: step(s + 1))
        send_out(1, aback, a_send, a_recv)

    def meet_copy(back, every, send, recv, r):
        return copy_to(back.at[:, r], every.at[pl.ds(o * 12, 12)], send.at[r], recv, orb=(r + z) % 8)

    def send_meet(back, every, send, recv):
        def one(r):
            @pl.when((r + z) % 8 != o)
            def _():
                meet_copy(back, every, send, recv, r).start()

            @pl.when((r + z) % 8 == o)
            def _():
                pltpu.make_async_copy(back.at[:, r], every.at[pl.ds(o * 12, 12)], recv).start()

        loop(6, one)

    def sent_meet(back, every, send, recv):
        def one(r):
            @pl.when((r + z) % 8 != o)
            def _():
                meet_copy(back, every, send, recv, r).wait_send()

        loop(6, one)

    landed(fback, f_recv)
    send_meet(fback, fall, rf_send, rf_recv)
    landed(aback, a_recv)
    send_meet(aback, aall, ra_send, ra_recv)

    meets = (o + 16 - z) % 8 < 6

    @pl.when(meets)
    def _():
        landed(fall, rf_recv)
        landed(aall, ra_recv)
        over = jnp.zeros((NORB, NORB), jnp.float32)
        proj = jnp.zeros((NORB, NORB), jnp.float32)
        dims = (((1,), (1,)), ((), ()))
        for s in range(8):
            f, a = fall[:, s, :], aall[:, s, :]
            over = over + lax.dot_general(f, f, dims, precision=HI, preferred_element_type=jnp.float32)
            proj = proj + lax.dot_general(f, a, dims, precision=HI, preferred_element_type=jnp.float32)
        gram_ref[...] = jnp.zeros_like(gram_ref)
        gram_ref[0:NORB, 0:NORB] = over
        gram_ref[NORB : 2 * NORB, 0:NORB] = proj
        fall_ref[...] = fall[...]

    @pl.when(jnp.logical_not(meets))
    def _():
        gram_ref[...] = jnp.zeros_like(gram_ref)
        fall_ref[...] = jnp.zeros_like(fall_ref)

    sent_meet(fback, fall, rf_send, rf_recv)
    sent_meet(aback, aall, ra_send, ra_recv)

    def sent_in(j):
        @pl.when(holder(j, y_lo) != d)
        def _():
            in_copy(j).wait_send()

            @pl.when(o < 6)
            def _():
                pot_copy(j).wait_send()

    loop(12, sent_in)

    @pl.when(active)
    def _():
        @pl.when(o < 6)
        def _():
            def one(b):
                @pl.when(b != o)
                def _():
                    share_copy(b).wait_send()

            loop(8, one)

        sent_out(0, fback, f_send, f_recv)
        sent_out(1, aback, a_send, a_recv)


def greet_groups(groups):
    barrier = pltpu.get_barrier_semaphore()
    for size, me, axes in groups:
        def one(b, me=me, axes=axes):
            @pl.when(b != me)
            def _():
                pl.semaphore_signal(barrier, inc=1, device_id=axes(b), device_id_type=MESH)

        loop(size, one)
    pl.semaphore_wait(barrier, sum(size - 1 for size, _, _ in groups))


def sum_kernel(g_ref, out_ref, part, ra, rb, rc, full, *sems):
    d, o = lax.axis_index("dom"), lax.axis_index("orb")
    low, high = d % 8, d // 8
    in_orb = (8, o, lambda b: {"orb": b})
    in_low = (8, low, lambda b: {"dom": high * 8 + b})
    in_high = (8, high, lambda b: {"dom": b * 8 + low})
    greet_groups((in_orb, in_low, in_high))
    waits = []

    def exchange(group, src, slots, send, recv):
        size, me, axes = group

        def each(do):
            def one(b):
                @pl.when(b != me)
                def _():
                    do(copy_to(src(b), slots.at[me], send.at[b], recv, **axes(b)))

            loop(size, one)

        each(lambda copy: copy.start())
        waits.append(lambda: each(lambda copy: copy.wait_send()))
        landed(slots.at[pl.ds(0, size - 1)], recv)

    def total(slots):
        acc = slots[0]
        for b in range(1, 8):
            acc = acc + slots[b]
        return acc

    mine = pl.multiple_of(o * 24, 8)
    ra[o] = g_ref[pl.ds(mine, 24), :]
    exchange(in_orb, lambda b: g_ref.at[pl.ds(pl.multiple_of(b * 24, 8), 24)], ra, sems[0], sems[1])
    part[0] = total(ra)
    rb[low] = part[0]
    exchange(in_low, lambda b: part.at[0], rb, sems[2], sems[3])
    part[1] = total(rb)
    rc[high] = part[1]
    exchange(in_high, lambda b: part.at[1], rc, sems[4], sems[5])
    part[2] = total(rc)
    full[o] = part[2]
    exchange(in_orb, lambda b: part.at[2], full, sems[6], sems[7])
    out_ref[...] = full[...].reshape(192, 128)
    for wait in waits:
        wait()


def rotate_kernel(inv_ref, fall_ref, out_ref, rot, send, recv):
    d, o = lax.axis_index("dom"), lax.axis_index("orb")
    z = (d // 2) % 16
    greet_groups(((8, o, lambda b: {"orb": b}),))
    r = (o + 16 - z) % 8

    def copy(b):
        return copy_to(rot.at[pl.ds(b * 12, 12)], out_ref.at[:, 0, r], send.at[b], recv, orb=b)

    @pl.when(r < 6)
    def _():
        inv = inv_ref[...]
        for s in range(8):
            rot[:, s, :] = jnp.dot(inv, fall_ref[:, s, :], precision=HI, preferred_element_type=jnp.float32)

        def one(b):
            @pl.when(b != o)
            def _():
                copy(b).start()

            @pl.when(b == o)
            def _():
                pltpu.make_async_copy(rot.at[pl.ds(b * 12, 12)], out_ref.at[:, 0, r], recv).start()

        loop(8, one)

    landed(out_ref, recv)

    @pl.when(r < 6)
    def _():
        def one(b):
            @pl.when(b != o)
            def _():
                copy(b).wait_send()

        loop(8, one)


def local(orbitals, potential):
    f32 = jnp.float32
    vmem, anyspace = pl.BlockSpec(memory_space=pltpu.VMEM), pl.BlockSpec(memory_space=pl.ANY)
    dma = pltpu.SemaphoreType.DMA
    fall, gram = pl.pallas_call(
        filter_kernel,
        out_shape=(
            jax.ShapeDtypeStruct((NORB, 8, 128), f32),
            jax.ShapeDtypeStruct((2 * NORB, 128), f32),
        ),
        in_specs=[pl.BlockSpec(memory_space=pltpu.SMEM), anyspace, anyspace, vmem],
        out_specs=(vmem, vmem),
        scratch_shapes=[
            pltpu.VMEM((2, EXT_ROWS, EXT_COLS, 128), f32),
            pltpu.VMEM((4, 6, 64, 128), f32),
            pltpu.VMEM((6, 64, 128), f32),
            pltpu.VMEM((12, 6, 8, 128), f32),
            pltpu.VMEM((12, 6, 8, 128), f32),
            pltpu.VMEM((NORB, 8, 128), f32),
            pltpu.VMEM((NORB, 8, 128), f32),
            dma((12,)), dma, dma((12,)), dma, dma((8,)), dma((6,)), dma((2,)), dma((2,)),
            dma((32,)), dma, dma((32,)), dma, dma((6,)), dma, dma((6,)), dma,
        ],
        compiler_params=pltpu.CompilerParams(
            collective_id=0, has_side_effects=True, vmem_limit_bytes=32 * 2**20
        ),
        name="filter_orbitals",
    )(jnp.asarray(step_scalars()), orbitals, potential, jnp.asarray(z_weights()))
    total = pl.pallas_call(
        sum_kernel,
        out_shape=jax.ShapeDtypeStruct((2 * NORB, 128), f32),
        in_specs=[vmem],
        out_specs=vmem,
        scratch_shapes=[pltpu.VMEM((3, 24, 128), f32)]
        + [pltpu.VMEM((8, 24, 128), f32)] * 4
        + [dma((8,)), dma] * 4,
        compiler_params=pltpu.CompilerParams(collective_id=1, has_side_effects=True),
        name="sum_over_devices",
    )(gram)
    intersection = total[:NORB, :NORB] / float(CELLS)
    projected = total[NORB:, :NORB] / float(CELLS)
    lower = jnp.linalg.cholesky(intersection)
    inverse = lax.linalg.triangular_solve(lower, jnp.eye(NORB, dtype=f32), left_side=True, lower=True)
    subspace_h = jnp.dot(jnp.dot(inverse, projected, precision=HI), inverse.T, precision=HI)
    rotated = pl.pallas_call(
        rotate_kernel,
        out_shape=jax.ShapeDtypeStruct(orbitals.shape, f32),
        in_specs=[vmem, vmem],
        out_specs=anyspace,
        scratch_shapes=[pltpu.VMEM((NORB, 8, 128), f32), dma((8,)), dma],
        compiler_params=pltpu.CompilerParams(collective_id=2, has_side_effects=True),
        name="rotate_orbitals",
    )(inverse, fall)
    return (rotated, subspace_h)


def solution(mesh):
    return jax.shard_map(
        local,
        mesh=mesh,
        in_specs=(P("orb", "dom", None, None, None), P("dom", None, None, None)),
        out_specs=(P("orb", "dom", None, None, None), P()),
        check_vma=False,
    )
```

```python
import jax
import jax.numpy as jnp
from jax import lax
from jax.experimental import pallas as pl
from jax.experimental.pallas import tpu as pltpu
from jax.sharding import PartitionSpec as P

MESH = pl.DeviceIdType.MESH
HI = lax.Precision.HIGHEST
F32 = jnp.float32

NORB = 96
DEGREE = 8
RADIUS = 6
CELLS = 48 * 64 * 128

COEF = (
    -5369.0 / 1800.0,
    12.0 / 7.0,
    -15.0 / 56.0,
    10.0 / 189.0,
    -1.0 / 112.0,
    2.0 / 1925.0,
    -1.0 / 16632.0,
)
E_HALF = 6.0
CENTER = 8.0
A_LOW = 0.0

ROWS = 24
EXT_ROWS = ROWS + 2 * RADIUS
EXT_COLS = 80


def step_scalars():
    rows = [(0.0, 0.0, 0.0)]
    sigma = sigma_one = E_HALF / (A_LOW - CENTER)
    rows.append((sigma_one / E_HALF, CENTER, 0.0))
    for _ in range(2, DEGREE + 1):
        sigma_next = 1.0 / (2.0 / sigma_one - sigma)
        rows.append((2.0 * sigma_next / E_HALF, CENTER, sigma * sigma_next))
        sigma = sigma_next
    rows.append((1.0, 0.0, 0.0))
    return rows


def holder(j, c):
    y_lo, slot = j % 2, j // 2
    return y_lo * 32 + ((slot * 8) // 3 + y_lo) * 2 + c


def copy_to(src, dst, send, recv, axes):
    return pltpu.make_async_remote_copy(
        src_ref=src, dst_ref=dst, send_sem=send, recv_sem=recv, device_id=axes, device_id_type=MESH
    )


def landed(ref, sem):
    pltpu.make_async_copy(ref, ref, sem).wait()


def loop(n, body):
    lax.fori_loop(0, n, lambda i, carry: (body(i), carry)[1], 0)


def when(cond):
    return pl.when(cond)


def over_lanes(tile, j):
    return jnp.broadcast_to(tile[:, j : j + 1], (8, 128))


def over_rows(tile, r):
    return jnp.broadcast_to(tile[r : r + 1, :], (8, 128))


def inverse_factor(matrix):
    sub = lax.broadcasted_iota(jnp.int32, (8, 128), 0)
    lane = lax.broadcasted_iota(jnp.int32, (8, 128), 1)
    tiles = NORB // 8
    st = [matrix[8 * t : 8 * t + 8, :] for t in range(tiles)]
    et = [jnp.where(lane == sub + 8 * t, 1.0, 0.0).astype(F32) for t in range(tiles)]
    for j in range(0, NORB, 2):
        t0, r = divmod(j, 8)
        c0 = [over_lanes(st[t], j) for t in range(t0, tiles)]
        c1 = [over_lanes(st[t], j + 1) for t in range(t0, tiles)]
        a, b, c = over_rows(c0[0], r), over_rows(c0[0], r + 1), over_rows(c1[0], r + 1)
        s0, s1 = over_rows(st[t0], r), over_rows(st[t0], r + 1)
        e0, e1 = over_rows(et[t0], r), over_rows(et[t0], r + 1)
        inv_a = 1.0 / a
        q = b * inv_a
        d = c - b * q
        inv_d = 1.0 / d
        s1 = (s1 - q * s0) * inv_d
        e1 = e1 - q * e0
        s0 = s0 * inv_a
        e0d, e1d = e0 * inv_a, e1 * inv_d
        for t in range(t0, tiles):
            m0 = c0[t - t0]
            m1 = c1[t - t0] - m0 * q
            if t == t0:
                m0, m1 = jnp.where(sub > r + 1, m0, 0.0), jnp.where(sub > r + 1, m1, 0.0)
            st[t] = st[t] - m0 * s0 - m1 * s1
            et[t] = et[t] - m0 * e0d - m1 * e1d
        et[t0] = jnp.where(
            sub == r, e0 * lax.rsqrt(a), jnp.where(sub == r + 1, e1 * lax.rsqrt(d), et[t0])
        )
    return jnp.concatenate(et, axis=0)


def kernel(
    orb_ref, pot_ref, out_ref, sub_ref,
    buf, potb, zs, w, scal, back, every, gram, r1, r2, mine, full, rot,
    in_send, in_recv, p_send, p_recv, g_send, g_recv, h_send, h_recv, b_send, b_recv, m_send, m_recv,
    r1_send, r1_recv, r2_send, r2_recv, r3_send, full_recv, o_send, o_recv,
):
    d, o = lax.axis_index("dom"), lax.axis_index("orb")
    y_lo, z, c = d // 32, (d // 2) % 16, d % 2
    prow, pcol = d // 8, d % 8
    off = jnp.maximum(z - y_lo, 0)
    slot = (off * 3 + 2) // 8
    active = (z >= y_lo) & (slot < 6) & ((slot * 8) // 3 == off)
    orbital = slot * 2 + y_lo
    selfpair = active & (c == y_lo)
    meet_row = (o + 16 - z) % 8
    meets = meet_row < 6
    tile = y_lo * 8 + o
    owns = tile < 12

    barrier = pltpu.get_barrier_semaphore()

    def greet(cond, axes):
        @when(cond)
        def _():
            pl.semaphore_signal(barrier, inc=1, device_id=axes, device_id_type=MESH)

    def start(here, src, dst, send, recv, axes):
        @when(here)
        def _():
            pltpu.make_async_copy(src, dst, recv).start()

        @when(jnp.logical_not(here))
        def _():
            copy_to(src, dst, send, recv, axes).start()

    def left(here, src, dst, send, recv, axes):
        @when(jnp.logical_not(here))
        def _():
            copy_to(src, dst, send, recv, axes).wait_send()

    @when(active)
    def _():
        loop(32, lambda m: greet(c * 32 + m != d, {"dom": c * 32 + m}))

    loop(12, lambda j: greet(holder(j, y_lo) != d, {"dom": holder(j, y_lo)}))
    loop(8, lambda b: greet(b != o, {"orb": b}))

    partner = {"dom": d + 1 - 2 * c}

    @when(active)
    def _():
        margin, side = jnp.zeros((EXT_COLS, 128), F32), jnp.zeros((8, 128), F32)

        def clear(i):
            buf[1, i] = margin
            buf[0, i, 0:8, :] = side
            buf[0, i, 72:80, :] = side

        loop(EXT_ROWS, clear)

        def clear_rows(i):
            buf[0, i] = margin
            buf[0, i + EXT_ROWS - RADIUS] = margin

        loop(RADIUS, clear_rows)
        gap = jnp.abs(
            lax.broadcasted_iota(jnp.int32, (128, 128), 0) - lax.broadcasted_iota(jnp.int32, (128, 128), 1)
        )
        weights = jnp.where(gap == 0, -1.5 * COEF[0], 0.0)
        for k in range(1, RADIUS + 1):
            weights = jnp.where(gap == k, -0.5 * COEF[k], weights)
        w[...] = weights.astype(F32)
        for s, row in enumerate(step_scalars()):
            for i, value in enumerate(row):
                scal[3 * s + i] = jnp.float32(value)
        greet(active, partner)

    pl.semaphore_wait(barrier, 19 + 33 * active.astype(jnp.int32) - 2 * selfpair.astype(jnp.int32))

    far = (((z + 8) % 16) * 3) // 4
    col0 = pl.multiple_of(pcol * 8, 8)

    def far_first(i):
        return (far + 12 + jnp.where(i % 2 == 0, -(i // 2), (i + 1) // 2)) % 12

    def pot_args(j):
        t = holder(j, y_lo)
        return t == d, pot_ref.at[0, o], potb.at[prow % 4, o, pl.ds(col0, 8)], p_send.at[j], p_recv.at[prow % 4], {"dom": t}

    def in_args(j):
        t = holder(j, y_lo)
        dst = buf.at[0, pl.ds(RADIUS + (prow % 4) * 6, 6), pl.ds(pl.multiple_of(8 + pcol * 8, 8), 8)]
        return t == d, orb_ref.at[j, 0], dst, in_send.at[j], in_recv, {"dom": t}

    @when(o < 6)
    def _():
        loop(12, lambda i: start(*pot_args(far_first(i))))

    loop(12, lambda i: start(*in_args(far_first(i))))

    def share_args(n):
        q, b = n // 8, n % 8
        return b == o, potb.at[q, o], potb.at[q, o], g_send.at[n], g_recv.at[o], {"orb": b}

    def out_args(at, m):
        q, col = m // 8, m % 8
        src = buf.at[at, pl.ds(RADIUS + q * 6, 6), pl.ds(pl.multiple_of(8 + col * 8, 8), 8)]
        t = c * 32 + m
        return t == d, src, back.at[at, orbital], b_send.at[at, m], b_recv.at[at], {"dom": t}

    @when(active)
    def _():
        @when(o < 6)
        def _():
            def share(i):
                q = (z // 4 + jnp.where(i == 2, 3, jnp.where(i == 3, 2, i))) % 4
                landed(potb.at[q, 0], p_recv.at[q])

                def one(b):
                    here, src, dst, send, recv, axes = share_args(q * 8 + b)

                    @when(jnp.logical_not(here))
                    def _():
                        copy_to(src, dst, send, recv, axes).start()

                loop(8, one)

            loop(4, share)

        def shared(r):
            @when(r != o)
            def _():
                landed(potb.at[:, 0], g_recv.at[r])

        loop(6, shared)
        landed(buf.at[0, pl.ds(RADIUS, ROWS), pl.ds(8, 64)], in_recv)

        def step(s):
            cur, new = (s + 1) % 2, s % 2
            halo = copy_to(
                buf.at[cur, pl.ds(24 - 18 * c, 6), pl.ds(8, 64)],
                buf.at[cur, pl.ds(30 * c, 6), pl.ds(8, 64)],
                h_send.at[cur], h_recv.at[cur], partner,
            )
            halo.start()
            scale, shift, past = scal[3 * s], scal[3 * s + 1], scal[3 * s + 2]

            def block(i):
                @when(i == 3)
                def _():
                    halo.wait_recv()

                blk = jnp.where(c == 0, i, 3 - i)
                r0 = RADIUS + blk * 6
                x = buf[cur, pl.ds(r0, 6), 8:72, :].reshape(6 * 64, 128)
                zs[...] = jnp.dot(x, w[...], precision=HI, preferred_element_type=F32).reshape(6, 64, 128)
                for yt in range(8):
                    y0 = 8 + 8 * yt
                    col = [buf[cur, r0 - RADIUS + m, y0 : y0 + 8, :] for m in range(18)]
                    for i6 in range(6):
                        r = r0 + i6
                        acc = zs[i6, y0 - 8 : y0, :]
                        mid = col[i6 + RADIUS]
                        for k in range(1, RADIUS + 1):
                            term = col[i6 + RADIUS + k] + col[i6 + RADIUS - k]
                            term = term + (
                                buf[cur, r, y0 + k : y0 + k + 8, :] + buf[cur, r, y0 - k : y0 - k + 8, :]
                            )
                            acc = acc + (-0.5 * COEF[k]) * term
                        acc = acc + (potb[blk, i6, y0 - 8 : y0, :] - shift) * mid
                        buf[new, r, y0 : y0 + 8, :] = scale * acc - past * buf[new, r, y0 : y0 + 8, :]

                @when(s >= DEGREE)
                def _():
                    loop(8, lambda col: start(*out_args(new, blk * 8 + col)))

            loop(4, block)
            halo.wait_send()

        loop(DEGREE + 1, lambda s: step(s + 1))

    def meet_args(what, r):
        b = (r + z) % 8
        dst = every.at[what, pl.ds(o * 12, 12)]
        return b == o, back.at[what, :, r], dst, m_send.at[what, r], m_recv.at[what], {"orb": b}

    def send_meet(what):
        landed(back.at[what], b_recv.at[what])
        loop(6, lambda r: start(*meet_args(what, r)))

    def r1_args(what, m):
        axes = {"orb": m % 8, "dom": (m // 8) * 32 + z * 2 + what}
        here = (tile == m) & (c == what)
        return here, gram.at[what, m], r1.at[meet_row * 4 + y_lo * 2 + c], r1_send.at[what, m], r1_recv, axes

    def r2_args(b):
        return b == z, mine.at[0], r2.at[z], r2_send.at[b], r2_recv, {"dom": y_lo * 32 + b * 2 + c}

    def r3_args(n):
        b, y, core = n // 4, (n // 2) % 2, n % 2
        here = (b == o) & (y == y_lo) & (core == c)
        axes = {"orb": b, "dom": y * 32 + z * 2 + core}
        return here, mine.at[1], full.at[c, tile], r3_send.at[n], full_recv.at[c], axes

    def meet_sums(what):
        @when(meets)
        def _():
            landed(every.at[what], m_recv.at[what])
            acc = jnp.zeros((NORB, NORB), F32)
            for s in range(8):
                acc = acc + lax.dot_general(
                    every[0, :, s, :], every[what, :, s, :], (((1,), (1,)), ((), ())),
                    precision=HI, preferred_element_type=F32,
                )
            for m in range(12):
                gram[what, m] = jnp.zeros((8, 128), F32)
                gram[what, m, :, 0:NORB] = acc[8 * m : 8 * m + 8, :]
            loop(12, lambda m: start(*r1_args(what, m)))

    def plane_sum(what):
        @when(owns & (c == what))
        def _():
            landed(r1, r1_recv)
            parts = [r1[b] for b in range(24)]
            while len(parts) > 1:
                parts = [sum(parts[i + 1 : i + 2], parts[i]) for i in range(0, len(parts), 2)]
            mine[0] = parts[0]
            loop(16, lambda b: start(*r2_args(b)))

    def whole_sum(what):
        @when(owns & (c == what))
        def _():
            landed(r2, r2_recv)
            parts = [r2[b] for b in range(16)]
            while len(parts) > 1:
                parts = [parts[i] + parts[i + 1] for i in range(0, len(parts), 2)]
            mine[1] = parts[0] * (1.0 / CELLS)
            loop(32, lambda n: start(*r3_args(n)))

    send_meet(0)
    meet_sums(0)
    send_meet(1)
    plane_sum(0)
    meet_sums(1)
    whole_sum(0)
    plane_sum(1)
    landed(full.at[0], full_recv.at[0])
    inverse = inverse_factor(full[0].reshape(NORB, 128))[:, :NORB]

    def o_args(b):
        dst = out_ref.at[:, 0, meet_row]
        return b == o, rot.at[pl.ds(b * 12, 12)], dst, o_send.at[b], o_recv, {"orb": b}

    @when(meets)
    def _():
        for s in range(8):
            rot[:, s, :] = jnp.dot(inverse, every[0, :, s, :], precision=HI, preferred_element_type=F32)
        loop(8, lambda b: start(*o_args(b)))

    whole_sum(1)
    landed(full.at[1], full_recv.at[1])
    projected = full[1].reshape(NORB, 128)[:, :NORB]
    half = jnp.dot(inverse, projected, precision=HI, preferred_element_type=F32)
    sub_ref[...] = lax.dot_general(
        half, inverse, (((1,), (1,)), ((), ())), precision=HI, preferred_element_type=F32
    )

    loop(12, lambda j: left(*in_args(j)))

    @when(o < 6)
    def _():
        loop(12, lambda j: left(*pot_args(j)))

    @when(active)
    def _():
        @when(o < 6)
        def _():
            loop(32, lambda n: left(*share_args(n)))

        loop(32, lambda m: left(*out_args(0, m)))
        loop(32, lambda m: left(*out_args(1, m)))

    for what in range(2):
        loop(6, lambda r: left(*meet_args(what, r)))

        @when(meets)
        def _():
            loop(12, lambda m: left(*r1_args(what, m)))

    @when(owns)
    def _():
        loop(16, lambda b: left(*r2_args(b)))
        loop(32, lambda n: left(*r3_args(n)))

    @when(meets)
    def _():
        loop(8, lambda b: left(*o_args(b)))

    landed(out_ref, o_recv)


def local(orbitals, potential):
    vmem, anyspace = pl.BlockSpec(memory_space=pltpu.VMEM), pl.BlockSpec(memory_space=pl.ANY)
    dma = pltpu.SemaphoreType.DMA
    return pl.pallas_call(
        kernel,
        out_shape=(
            jax.ShapeDtypeStruct(orbitals.shape, F32),
            jax.ShapeDtypeStruct((NORB, NORB), F32),
        ),
        in_specs=[anyspace, anyspace],
        out_specs=(anyspace, vmem),
        scratch_shapes=[
            pltpu.VMEM((2, EXT_ROWS, EXT_COLS, 128), F32),
            pltpu.VMEM((4, 6, 64, 128), F32),
            pltpu.VMEM((6, 64, 128), F32),
            pltpu.VMEM((128, 128), F32),
            pltpu.SMEM((32,), F32),
            pltpu.VMEM((2, 12, 6, 8, 128), F32),
            pltpu.VMEM((2, NORB, 8, 128), F32),
            pltpu.VMEM((2, 12, 8, 128), F32),
            pltpu.VMEM((24, 8, 128), F32),
            pltpu.VMEM((16, 8, 128), F32),
            pltpu.VMEM((2, 8, 128), F32),
            pltpu.VMEM((2, 12, 8, 128), F32),
            pltpu.VMEM((NORB, 8, 128), F32),
            dma((12,)), dma, dma((12,)), dma((4,)), dma((32,)), dma((6,)), dma((2,)), dma((2,)),
            dma((2, 32)), dma((2,)), dma((2, 6)), dma((2,)),
            dma((2, 12)), dma, dma((16,)), dma, dma((32,)), dma((2,)), dma((8,)), dma,
        ],
        compiler_params=pltpu.CompilerParams(
            collective_id=0, has_side_effects=True, vmem_limit_bytes=60 * 2**20
        ),
        name="filter_and_rotate",
    )(orbitals, potential)


def solution(mesh):
    return jax.shard_map(
        local,
        mesh=mesh,
        in_specs=(P("orb", "dom", None, None, None), P("dom", None, None, None)),
        out_specs=(P("orb", "dom", None, None, None), P()),
        check_vma=False,
    )
```

```python
import jax
import jax.numpy as jnp
from jax import lax
from jax.experimental import pallas as pl
from jax.experimental.pallas import tpu as pltpu
from jax.sharding import PartitionSpec as P

MESH = pl.DeviceIdType.MESH
HI = lax.Precision.HIGHEST
F32 = jnp.float32

NORB = 96
DEGREE = 8
RADIUS = 6
CELLS = 48 * 64 * 128

COEF = (
    -5369.0 / 1800.0,
    12.0 / 7.0,
    -15.0 / 56.0,
    10.0 / 189.0,
    -1.0 / 112.0,
    2.0 / 1925.0,
    -1.0 / 16632.0,
)
E_HALF = 6.0
CENTER = 8.0
A_LOW = 0.0

ROWS = 24
EXT_ROWS = ROWS + 2 * RADIUS
EXT_COLS = 80


def step_scalars():
    rows = [(0.0, 0.0, 0.0)]
    sigma = sigma_one = E_HALF / (A_LOW - CENTER)
    rows.append((sigma_one / E_HALF, CENTER, 0.0))
    for _ in range(2, DEGREE + 1):
        sigma_next = 1.0 / (2.0 / sigma_one - sigma)
        rows.append((2.0 * sigma_next / E_HALF, CENTER, sigma * sigma_next))
        sigma = sigma_next
    rows.append((1.0, 0.0, 0.0))
    return [(scale, center + 1.5 * COEF[0], past) for scale, center, past in rows]


def holder(j, c):
    y_lo, slot = j % 2, j // 2
    return y_lo * 32 + ((slot * 8) // 3 + y_lo) * 2 + c


def copy_to(src, dst, send, recv, axes):
    return pltpu.make_async_remote_copy(
        src_ref=src, dst_ref=dst, send_sem=send, recv_sem=recv, device_id=axes, device_id_type=MESH
    )


def landed(ref, sem):
    pltpu.make_async_copy(ref, ref, sem).wait()


def loop(n, body):
    lax.fori_loop(0, n, lambda i, carry: (body(i), carry)[1], 0)


def when(cond):
    return pl.when(cond)


def over_lanes(tile, j):
    return jnp.broadcast_to(tile[:, j : j + 1], (8, 128))


def over_rows(tile, r):
    return jnp.broadcast_to(tile[r : r + 1, :], (8, 128))


def inverse_factor(matrix):
    sub = lax.broadcasted_iota(jnp.int32, (8, 128), 0)
    lane = lax.broadcasted_iota(jnp.int32, (8, 128), 1)
    tiles = NORB // 8
    st = [matrix[8 * t : 8 * t + 8, :] for t in range(tiles)]
    et = [jnp.where(lane == sub + 8 * t, 1.0, 0.0).astype(F32) for t in range(tiles)]
    for j in range(0, NORB, 2):
        t0, r = divmod(j, 8)
        c0 = [over_lanes(st[t], j) for t in range(t0, tiles)]
        c1 = [over_lanes(st[t], j + 1) for t in range(t0, tiles)]
        a, b, c = over_rows(c0[0], r), over_rows(c0[0], r + 1), over_rows(c1[0], r + 1)
        s0, s1 = over_rows(st[t0], r), over_rows(st[t0], r + 1)
        e0, e1 = over_rows(et[t0], r), over_rows(et[t0], r + 1)
        inv_a = 1.0 / a
        q = b * inv_a
        d = c - b * q
        inv_d = 1.0 / d
        s1 = (s1 - q * s0) * inv_d
        e1 = e1 - q * e0
        s0 = s0 * inv_a
        e0d, e1d = e0 * inv_a, e1 * inv_d
        for t in range(t0, tiles):
            m0 = c0[t - t0]
            m1 = c1[t - t0] - m0 * q
            if t == t0:
                m0, m1 = jnp.where(sub > r + 1, m0, 0.0), jnp.where(sub > r + 1, m1, 0.0)
            st[t] = st[t] - m0 * s0 - m1 * s1
            et[t] = et[t] - m0 * e0d - m1 * e1d
        et[t0] = jnp.where(
            sub == r, e0 * lax.rsqrt(a), jnp.where(sub == r + 1, e1 * lax.rsqrt(d), et[t0])
        )
    return jnp.concatenate(et, axis=0)


def kernel(
    orb_ref, pot_ref, out_ref, sub_ref,
    buf0, buf1, potb, w, scal, every, gram, r1, r2, mine, full, rot,
    in_send, in_recv, p_send, p_recv, g_send, g_recv, h_send, h_recv, m_send, m_recv, mates,
    r1_send, r1_recv, r2_send, r2_recv, r3_send, full_recv, o_send, o_recv,
):
    d, o = lax.axis_index("dom"), lax.axis_index("orb")
    y_lo, z, c = d // 32, (d // 2) % 16, d % 2
    prow, pcol = d // 8, d % 8
    off = jnp.maximum(z - y_lo, 0)
    slot = (off * 3 + 2) // 8
    active = (z >= y_lo) & (slot < 6) & ((slot * 8) // 3 == off)
    orbital = slot * 2 + y_lo
    selfpair = active & (c == y_lo)
    meet_row = (o + 16 - z) % 8
    meets = meet_row < 6
    tile = y_lo * 8 + o
    owns = tile < 12

    barrier = pltpu.get_barrier_semaphore()

    def greet(cond, axes):
        @when(cond)
        def _():
            pl.semaphore_signal(barrier, inc=1, device_id=axes, device_id_type=MESH)

    def start(here, src, dst, send, recv, axes):
        @when(here)
        def _():
            pltpu.make_async_copy(src, dst, recv).start()

        @when(jnp.logical_not(here))
        def _():
            copy_to(src, dst, send, recv, axes).start()

    def left(here, src, dst, send, recv, axes):
        @when(jnp.logical_not(here))
        def _():
            copy_to(src, dst, send, recv, axes).wait_send()

    @when(active)
    def _():
        def source(i):
            m = c * 32 + (2 * z + 16 + jnp.where(i % 2 == 0, 32 - i // 2, (i + 1) // 2)) % 32
            greet(m != d, {"dom": m})

        loop(32, source)

    loop(8, lambda b: greet(b != o, {"orb": b}))

    partner = {"dom": d + 1 - 2 * c}

    @when(active)
    def _():
        margin, side = jnp.zeros((EXT_COLS, 128), F32), jnp.zeros((8, 128), F32)

        def clear(i):
            buf1[i] = margin
            buf0[i, 0:8, :] = side
            buf0[i, 72:80, :] = side

        loop(EXT_ROWS, clear)

        def clear_rows(i):
            buf0[i] = margin
            buf0[i + EXT_ROWS - RADIUS] = margin

        loop(RADIUS, clear_rows)
        gap = jnp.abs(
            lax.broadcasted_iota(jnp.int32, (128, 128), 0) - lax.broadcasted_iota(jnp.int32, (128, 128), 1)
        )
        weights = jnp.zeros((128, 128), F32)
        for k in range(1, RADIUS + 1):
            weights = jnp.where(gap == k, -0.5 * COEF[k], weights)
        high = weights.astype(jnp.bfloat16)
        low = (weights - high.astype(F32)).astype(jnp.bfloat16)
        for i in range(2):
            w[128 * i : 128 * i + 128, 0:128] = high
            w[128 * i : 128 * i + 128, 128:256] = low
        for s, row in enumerate(step_scalars()):
            for i, value in enumerate(row):
                scal[3 * s + i] = jnp.float32(value)
        greet(active, partner)

    pl.semaphore_wait(barrier, 19 + active.astype(jnp.int32) - selfpair.astype(jnp.int32))

    far = (((z + 8) % 16) * 3) // 4
    col0 = pl.multiple_of(pcol * 8, 8)

    def far_first(i):
        return (far + 12 + jnp.where(i % 2 == 0, -(i // 2), (i + 1) // 2)) % 12

    def pot_args(j):
        t = holder(j, y_lo)
        return t == d, pot_ref.at[0, o], potb.at[prow % 4, o, pl.ds(col0, 8)], p_send.at[j], p_recv.at[prow % 4], {"dom": t}

    def in_args(j):
        t = holder(j, y_lo)
        dst = buf0.at[pl.ds(RADIUS + (prow % 4) * 6, 6), pl.ds(pl.multiple_of(8 + pcol * 8, 8), 8)]
        return t == d, orb_ref.at[j, 0], dst, in_send.at[j], in_recv, {"dom": t}

    @when(o < 6)
    def _():
        loop(12, lambda i: start(*pot_args(far_first(i))))

    loop(12, lambda i: start(*in_args(far_first(i))))

    def share_args(n):
        q, b = n // 8, n % 8
        return b == o, potb.at[q, o], potb.at[q, o], g_send.at[n], g_recv.at[o], {"orb": b}

    def out_args(what, m, r):
        src = (buf0, buf1)[what].at[RADIUS + (m // 8) * 6 + r, pl.ds(pl.multiple_of(8 + (m % 8) * 8, 8), 8)]
        t = c * 32 + m
        b = (r + m // 2) % 8
        axes = {"orb": b, "dom": t}
        return (t == d) & (b == o), src, every.at[what, o * 12 + orbital], m_send.at[what, m], m_recv.at[what], axes

    @when(active)
    def _():
        @when(o < 6)
        def _():
            def share(i):
                q = (z // 4 + jnp.where(i == 2, 3, jnp.where(i == 3, 2, i))) % 4
                landed(potb.at[q, 0], p_recv.at[q])

                def one(b):
                    here, src, dst, send, recv, axes = share_args(q * 8 + b)

                    @when(jnp.logical_not(here))
                    def _():
                        copy_to(src, dst, send, recv, axes).start()

                loop(8, one)

            loop(4, share)

        def shared(r):
            @when(r != o)
            def _():
                landed(potb.at[:, 0], g_recv.at[r])

        loop(6, shared)
        landed(buf0.at[pl.ds(RADIUS, ROWS), pl.ds(8, 64)], in_recv)

        def tell(b):
            @when(b != o)
            def _():
                pl.semaphore_signal(mates, inc=1, device_id={"orb": b}, device_id_type=MESH)

        loop(8, tell)

        def step(s, what, cur, new, send):
            halo = copy_to(
                cur.at[pl.ds(24 - 18 * c, 6), pl.ds(8, 64)],
                cur.at[pl.ds(30 * c, 6), pl.ds(8, 64)],
                h_send.at[what], h_recv.at[what], partner,
            )
            halo.start()
            scale, shift, past = scal[3 * s], scal[3 * s + 1], scal[3 * s + 2]
            x = cur[RADIUS : RADIUS + ROWS, 8:72, :].reshape(ROWS * 64, 128)
            high = x.astype(jnp.bfloat16)
            low = (x - high.astype(F32)).astype(jnp.bfloat16)
            along = jnp.dot(jnp.concatenate([high, low], axis=1), w[...], preferred_element_type=F32)
            along = (along[:, :128] + along[:, 128:]).reshape(ROWS, 64, 128)
            new[RADIUS : RADIUS + ROWS, 8:72, :] = scale * along - past * new[RADIUS : RADIUS + ROWS, 8:72, :]

            def block(i):
                @when(i == 3)
                def _():
                    halo.wait_recv()

                blk = jnp.where(c == 0, i, 3 - i)
                r0 = RADIUS + blk * 6
                for yt in range(8):
                    y0 = 8 + 8 * yt
                    col = [cur[r0 - RADIUS + m, y0 : y0 + 8, :] for m in range(18)]
                    for i6 in range(6):
                        r = r0 + i6
                        mid = col[i6 + RADIUS]
                        acc = (potb[blk, i6, y0 - 8 : y0, :] - shift) * mid
                        for k in range(1, RADIUS + 1):
                            term = col[i6 + RADIUS + k] + col[i6 + RADIUS - k]
                            term = term + (cur[r, y0 + k : y0 + k + 8, :] + cur[r, y0 - k : y0 - k + 8, :])
                            acc = acc + (-0.5 * COEF[k]) * term
                        new[r, y0 : y0 + 8, :] = scale * acc + new[r, y0 : y0 + 8, :]

                @when(send)
                def _():
                    def row(n):
                        start(*out_args(1 - what, blk * 8 + n // 6, n % 6))

                    loop(48, row)

            loop(4, block)
            halo.wait_send()

        def two_steps(i):
            step(2 * i + 1, 0, buf0, buf1, i == 4)

            @when(i < 4)
            def _():
                @when(i == 3)
                def _():
                    pl.semaphore_wait(mates, 7)

                step(2 * i + 2, 1, buf1, buf0, i == 3)

        loop(5, two_steps)

    def r1_args(what, m):
        axes = {"orb": m % 8, "dom": (m // 8) * 32 + z * 2 + what}
        here = (tile == m) & (c == what)
        return here, gram.at[what, m], r1.at[meet_row * 4 + y_lo * 2 + c], r1_send.at[what, m], r1_recv, axes

    def r2_args(b):
        return b == z, mine.at[0], r2.at[z], r2_send.at[b], r2_recv, {"dom": y_lo * 32 + b * 2 + c}

    def r3_args(n):
        b, y, core = n // 4, (n // 2) % 2, n % 2
        here = (b == o) & (y == y_lo) & (core == c)
        axes = {"orb": b, "dom": y * 32 + z * 2 + core}
        return here, mine.at[1], full.at[c, tile], r3_send.at[n], full_recv.at[c], axes

    def meet_sums(what):
        @when(meets)
        def _():
            landed(every.at[what], m_recv.at[what])
            acc = jnp.zeros((NORB, NORB), F32)
            for s in range(8):
                acc = acc + lax.dot_general(
                    every[0, :, s, :], every[what, :, s, :], (((1,), (1,)), ((), ())),
                    precision=HI, preferred_element_type=F32,
                )
            for m in range(12):
                gram[what, m] = jnp.zeros((8, 128), F32)
                gram[what, m, :, 0:NORB] = acc[8 * m : 8 * m + 8, :]
            loop(12, lambda m: start(*r1_args(what, m)))

    def plane_sum(what):
        @when(owns & (c == what))
        def _():
            landed(r1, r1_recv)
            parts = [r1[b] for b in range(24)]
            while len(parts) > 1:
                parts = [sum(parts[i + 1 : i + 2], parts[i]) for i in range(0, len(parts), 2)]
            mine[0] = parts[0]
            loop(16, lambda b: start(*r2_args(b)))

    def whole_sum(what):
        @when(owns & (c == what))
        def _():
            landed(r2, r2_recv)
            parts = [r2[b] for b in range(16)]
            while len(parts) > 1:
                parts = [parts[i] + parts[i + 1] for i in range(0, len(parts), 2)]
            mine[1] = parts[0] * (1.0 / CELLS)
            loop(32, lambda n: start(*r3_args(n)))

    meet_sums(0)
    plane_sum(0)
    meet_sums(1)
    whole_sum(0)
    plane_sum(1)
    landed(full.at[0], full_recv.at[0])
    inverse = inverse_factor(full[0].reshape(NORB, 128))[:, :NORB]

    def o_args(b):
        dst = out_ref.at[:, 0, meet_row]
        return b == o, rot.at[pl.ds(b * 12, 12)], dst, o_send.at[b], o_recv, {"orb": b}

    @when(meets)
    def _():
        for s in range(8):
            rot[:, s, :] = jnp.dot(inverse, every[0, :, s, :], precision=HI, preferred_element_type=F32)
        loop(8, lambda b: start(*o_args(b)))

    whole_sum(1)
    landed(full.at[1], full_recv.at[1])
    projected = full[1].reshape(NORB, 128)[:, :NORB]
    half = jnp.dot(inverse, projected, precision=HI, preferred_element_type=F32)
    sub_ref[...] = lax.dot_general(
        half, inverse, (((1,), (1,)), ((), ())), precision=HI, preferred_element_type=F32
    )

    loop(12, lambda j: left(*in_args(j)))

    @when(o < 6)
    def _():
        loop(12, lambda j: left(*pot_args(j)))

    @when(active)
    def _():
        @when(o < 6)
        def _():
            loop(32, lambda n: left(*share_args(n)))

        for what in range(2):
            def gone(m):
                alone = (c * 32 + m == d) & meets

                @when(alone)
                def _():
                    landed(every.at[what, pl.ds(0, 5)], m_send.at[what, m])

                @when(jnp.logical_not(alone))
                def _():
                    landed(every.at[what, pl.ds(0, 6)], m_send.at[what, m])

            loop(32, gone)

    for what in range(2):

        @when(meets)
        def _():
            loop(12, lambda m: left(*r1_args(what, m)))

    @when(owns)
    def _():
        loop(16, lambda b: left(*r2_args(b)))
        loop(32, lambda n: left(*r3_args(n)))

    @when(meets)
    def _():
        loop(8, lambda b: left(*o_args(b)))

    landed(out_ref, o_recv)


def local(orbitals, potential):
    vmem, anyspace = pl.BlockSpec(memory_space=pltpu.VMEM), pl.BlockSpec(memory_space=pl.ANY)
    dma = pltpu.SemaphoreType.DMA
    return pl.pallas_call(
        kernel,
        out_shape=(
            jax.ShapeDtypeStruct(orbitals.shape, F32),
            jax.ShapeDtypeStruct((NORB, NORB), F32),
        ),
        in_specs=[anyspace, anyspace],
        out_specs=(anyspace, vmem),
        scratch_shapes=[
            pltpu.VMEM((EXT_ROWS, EXT_COLS, 128), F32),
            pltpu.VMEM((EXT_ROWS, EXT_COLS, 128), F32),
            pltpu.VMEM((4, 6, 64, 128), F32),
            pltpu.VMEM((256, 256), jnp.bfloat16),
            pltpu.SMEM((32,), F32),
            pltpu.VMEM((2, NORB, 8, 128), F32),
            pltpu.VMEM((2, 12, 8, 128), F32),
            pltpu.VMEM((24, 8, 128), F32),
            pltpu.VMEM((16, 8, 128), F32),
            pltpu.VMEM((2, 8, 128), F32),
            pltpu.VMEM((2, 12, 8, 128), F32),
            pltpu.VMEM((NORB, 8, 128), F32),
            dma((12,)), dma, dma((12,)), dma((4,)), dma((32,)), dma((6,)), dma((2,)), dma((2,)),
            dma((2, 32)), dma((2,)), pltpu.SemaphoreType.REGULAR,
            dma((2, 12)), dma, dma((16,)), dma, dma((32,)), dma((2,)), dma((8,)), dma,
        ],
        compiler_params=pltpu.CompilerParams(
            collective_id=0, has_side_effects=True, vmem_limit_bytes=60 * 2**20
        ),
        name="filter_and_rotate",
    )(orbitals, potential)


def solution(mesh):
    return jax.shard_map(
        local,
        mesh=mesh,
        in_specs=(P("orb", "dom", None, None, None), P("dom", None, None, None)),
        out_specs=(P("orb", "dom", None, None, None), P()),
        check_vma=False,
    )
```

```python
import jax
import jax.numpy as jnp
from jax import lax
from jax.experimental import pallas as pl
from jax.experimental.pallas import tpu as pltpu
from jax.sharding import PartitionSpec as P

MESH = pl.DeviceIdType.MESH
HI = lax.Precision.HIGHEST
F32 = jnp.float32

NORB = 96
DEGREE = 8
RADIUS = 6
CELLS = 48 * 64 * 128

COEF = (
    -5369.0 / 1800.0,
    12.0 / 7.0,
    -15.0 / 56.0,
    10.0 / 189.0,
    -1.0 / 112.0,
    2.0 / 1925.0,
    -1.0 / 16632.0,
)
E_HALF = 6.0
CENTER = 8.0
A_LOW = 0.0

ROWS = 24
EXT_ROWS = ROWS + 2 * RADIUS
EXT_COLS = 80

PAUSE = 92


def step_scalars():
    rows = [(0.0, 0.0, 0.0)]
    sigma = sigma_one = E_HALF / (A_LOW - CENTER)
    rows.append((sigma_one / E_HALF, CENTER, 0.0))
    for _ in range(2, DEGREE + 1):
        sigma_next = 1.0 / (2.0 / sigma_one - sigma)
        rows.append((2.0 * sigma_next / E_HALF, CENTER, sigma * sigma_next))
        sigma = sigma_next
    rows.append((1.0, 0.0, 0.0))
    return [(scale, center + 1.5 * COEF[0], past) for scale, center, past in rows]


def holder(j, c):
    y_lo, slot = j % 2, j // 2
    return y_lo * 32 + ((slot * 8) // 3 + y_lo) * 2 + c


def copy_to(src, dst, send, recv, axes):
    return pltpu.make_async_remote_copy(
        src_ref=src, dst_ref=dst, send_sem=send, recv_sem=recv, device_id=axes, device_id_type=MESH
    )


def landed(ref, sem):
    pltpu.make_async_copy(ref, ref, sem).wait()


def loop(n, body):
    lax.fori_loop(0, n, lambda i, carry: (body(i), carry)[1], 0)


def when(cond):
    return pl.when(cond)


def over_lanes(tile, j):
    return jnp.broadcast_to(tile[:, j : j + 1], (8, 128))


def over_rows(tile, r):
    return jnp.broadcast_to(tile[r : r + 1, :], (8, 128))


def inverse_factor(matrix, pause_at, pause):
    wide = 4
    sub = lax.broadcasted_iota(jnp.int32, (8, 128), 0)
    lane = lax.broadcasted_iota(jnp.int32, (8, 128), 1)
    tiles = NORB // 8
    st = [matrix[8 * t : 8 * t + 8, :] for t in range(tiles)]
    et = [jnp.where(lane == sub + 8 * t, 1.0, 0.0).astype(F32) for t in range(tiles)]
    for j in range(0, NORB, wide):
        if j == pause_at:
            pause()
        t0, r = divmod(j, 8)
        cols = [[over_lanes(st[t], j + k) for k in range(wide)] for t in range(t0, tiles)]
        a = {(k, q): over_rows(cols[0][q], r + k) for k in range(wide) for q in range(k + 1)}
        inv, low = [], {}
        for p in range(wide):
            inv.append(1.0 / a[p, p])
            for k in range(p + 1, wide):
                low[k, p] = a[k, p] * inv[p]
            for k in range(p + 1, wide):
                for q in range(p + 1, k + 1):
                    a[k, q] = a[k, q] - low[k, p] * a[q, p]

        def forward(rows):
            done = []
            for k, row in enumerate(rows):
                for p in range(k):
                    row = row - low[k, p] * done[p]
                done.append(row)
            return done

        srow = forward([over_rows(st[t0], r + k) for k in range(wide)])
        erow = forward([over_rows(et[t0], r + k) for k in range(wide)])
        sdiv = [row * i for row, i in zip(srow, inv)]
        ediv = [row * i for row, i in zip(erow, inv)]
        for t in range(t0, tiles):
            if t == t0 and r + wide == 8:
                continue
            mult = []
            for k in range(wide):
                col = cols[t - t0][k]
                for p in range(k):
                    col = col - mult[p] * low[k, p]
                mult.append(col)
            if t == t0:
                mult = [jnp.where(sub >= r + wide, col, 0.0) for col in mult]
            for k in range(wide):
                st[t] = st[t] - mult[k] * sdiv[k]
                et[t] = et[t] - mult[k] * ediv[k]
        for k in range(wide):
            et[t0] = jnp.where(sub == r + k, erow[k] * lax.rsqrt(a[k, k]), et[t0])
    return jnp.concatenate(et, axis=0)


def kernel(
    orb_ref, pot_ref, out_ref, sub_ref,
    buf0, buf1, potb, w, scal, every, gram, r1, r2, mine, full, rot, sub,
    in_send, in_recv, p_send, p_recv, g_send, g_recv, h_send, h_recv, m_send, m_recv, mates,
    r1_send, r1_recv, r2_send, r2_recv, r3_send, full_recv, o_send, o_recv, sub_sem,
):
    d, o = lax.axis_index("dom"), lax.axis_index("orb")
    y_lo, z, c = d // 32, (d // 2) % 16, d % 2
    prow, pcol = d // 8, d % 8
    off = jnp.maximum(z - y_lo, 0)
    slot = (off * 3 + 2) // 8
    active = (z >= y_lo) & (slot < 6) & ((slot * 8) // 3 == off)
    orbital = slot * 2 + y_lo
    selfpair = active & (c == y_lo)
    meet_row = (o + 16 - z) % 8
    meets = meet_row < 6
    tile = y_lo * 8 + o
    owns = tile < 12

    barrier = pltpu.get_barrier_semaphore()

    def greet(cond, axes):
        @when(cond)
        def _():
            pl.semaphore_signal(barrier, inc=1, device_id=axes, device_id_type=MESH)

    def start(here, src, dst, send, recv, axes):
        @when(here)
        def _():
            pltpu.make_async_copy(src, dst, recv).start()

        @when(jnp.logical_not(here))
        def _():
            copy_to(src, dst, send, recv, axes).start()

    def left(here, src, dst, send, recv, axes):
        @when(jnp.logical_not(here))
        def _():
            copy_to(src, dst, send, recv, axes).wait_send()

    @when(active)
    def _():
        def source(i):
            m = c * 32 + (2 * z + 16 + jnp.where(i % 2 == 0, 32 - i // 2, (i + 1) // 2)) % 32
            greet(m != d, {"dom": m})

        loop(32, source)

    loop(8, lambda b: greet(b != o, {"orb": b}))

    partner = {"dom": d + 1 - 2 * c}

    @when(active)
    def _():
        margin, side = jnp.zeros((EXT_COLS, 128), F32), jnp.zeros((8, 128), F32)

        def clear(i):
            buf1[i] = margin
            buf0[i, 0:8, :] = side
            buf0[i, 72:80, :] = side

        loop(EXT_ROWS, clear)

        def clear_rows(i):
            buf0[i] = margin
            buf0[i + EXT_ROWS - RADIUS] = margin

        loop(RADIUS, clear_rows)
        gap = jnp.abs(
            lax.broadcasted_iota(jnp.int32, (128, 128), 0) - lax.broadcasted_iota(jnp.int32, (128, 128), 1)
        )
        weights = jnp.zeros((128, 128), F32)
        for k in range(1, RADIUS + 1):
            weights = jnp.where(gap == k, -0.5 * COEF[k], weights)
        high = weights.astype(jnp.bfloat16)
        rest = weights - high.astype(F32)
        middle = rest.astype(jnp.bfloat16)
        low = (rest - middle.astype(F32)).astype(jnp.bfloat16)
        for i, row in enumerate(((high, middle, high), (high, middle, low))):
            for n, part in enumerate(row):
                w[128 * i : 128 * i + 128, 128 * n : 128 * n + 128] = part
        for s, row in enumerate(step_scalars()):
            for i, value in enumerate(row):
                scal[3 * s + i] = jnp.float32(value)
        greet(active, partner)

    pl.semaphore_wait(barrier, 19 + active.astype(jnp.int32) - selfpair.astype(jnp.int32))

    far = (((z + 8) % 16) * 3) // 4
    col0 = pl.multiple_of(pcol * 8, 8)

    def far_first(i):
        return (far + 12 + jnp.where(i % 2 == 0, -(i // 2), (i + 1) // 2)) % 12

    def pot_args(j):
        t = holder(j, y_lo)
        return t == d, pot_ref.at[0, o], potb.at[prow % 4, o, pl.ds(col0, 8)], p_send.at[j], p_recv.at[prow % 4], {"dom": t}

    def in_args(j):
        t = holder(j, y_lo)
        dst = buf0.at[pl.ds(RADIUS + (prow % 4) * 6, 6), pl.ds(pl.multiple_of(8 + pcol * 8, 8), 8)]
        return t == d, orb_ref.at[j, 0], dst, in_send.at[j], in_recv, {"dom": t}

    @when(o < 6)
    def _():
        loop(12, lambda i: start(*pot_args(far_first(i))))

    def send_in():
        loop(12, lambda i: start(*in_args(far_first(i))))

    @when(jnp.logical_not(active))
    def _():
        send_in()


    def share_args(n):
        q, b = n // 8, n % 8
        return b == o, potb.at[q, o], potb.at[q, o], g_send.at[n], g_recv.at[o], {"orb": b}

    def out_args(what, m, r):
        src = (buf0, buf1)[what].at[RADIUS + (m // 8) * 6 + r, pl.ds(pl.multiple_of(8 + (m % 8) * 8, 8), 8)]
        t = c * 32 + m
        b = (r + m // 2) % 8
        axes = {"orb": b, "dom": t}
        return (t == d) & (b == o), src, every.at[what, o * 12 + orbital], m_send.at[what, m], m_recv.at[what], axes

    def gone(what):
        def one(m):
            alone = (c * 32 + m == d) & meets

            @when(alone)
            def _():
                landed(every.at[what, pl.ds(0, 5)], m_send.at[what, m])

            @when(jnp.logical_not(alone))
            def _():
                landed(every.at[what, pl.ds(0, 6)], m_send.at[what, m])

        loop(32, one)

    @when(active)
    def _():
        @when(o < 6)
        def _():
            def share(i):
                q = (z // 4 + jnp.where(i == 2, 3, jnp.where(i == 3, 2, i))) % 4
                landed(potb.at[q, 0], p_recv.at[q])

                def one(b):
                    here, src, dst, send, recv, axes = share_args(q * 8 + b)

                    @when(jnp.logical_not(here))
                    def _():
                        copy_to(src, dst, send, recv, axes).start()

                loop(8, one)

            loop(4, share)

        send_in()

        def shared(r):
            @when(r != o)
            def _():
                landed(potb.at[:, 0], g_recv.at[r])

        loop(6, shared)
        landed(buf0.at[pl.ds(RADIUS, ROWS), pl.ds(8, 64)], in_recv)

        def tell(b):
            @when(b != o)
            def _():
                pl.semaphore_signal(mates, inc=1, device_id={"orb": b}, device_id_type=MESH)

        loop(8, tell)

        def step(s, what, cur, new, send):
            halo = copy_to(
                cur.at[pl.ds(24 - 18 * c, 6), pl.ds(8, 64)],
                cur.at[pl.ds(30 * c, 6), pl.ds(8, 64)],
                h_send.at[what], h_recv.at[what], partner,
            )
            halo.start()
            scale, shift, past = scal[3 * s], scal[3 * s + 1], scal[3 * s + 2]
            x = cur[RADIUS : RADIUS + ROWS, 8:72, :].reshape(ROWS * 64, 128)
            high = x.astype(jnp.bfloat16)
            rest = x - high.astype(F32)
            middle = rest.astype(jnp.bfloat16)
            low = (rest - middle.astype(F32)).astype(jnp.bfloat16)
            most = jnp.dot(jnp.concatenate([high, middle], axis=1), w[:, :256], preferred_element_type=F32)
            small = jnp.dot(jnp.concatenate([low, high], axis=1), w[:, 256:], preferred_element_type=F32)
            along = ((most[:, 128:] + small) + most[:, :128]).reshape(ROWS, 64, 128)
            new[RADIUS : RADIUS + ROWS, 8:72, :] = scale * along - past * new[RADIUS : RADIUS + ROWS, 8:72, :]

            def block(i):
                @when(i == 3)
                def _():
                    halo.wait_recv()

                blk = jnp.where(c == 0, i, 3 - i)
                r0 = RADIUS + blk * 6
                for yt in range(8):
                    y0 = 8 + 8 * yt
                    col = [cur[r0 - RADIUS + m, y0 : y0 + 8, :] for m in range(18)]
                    for i6 in range(6):
                        r = r0 + i6
                        mid = col[i6 + RADIUS]
                        acc = (potb[blk, i6, y0 - 8 : y0, :] - shift) * mid
                        for k in range(1, RADIUS + 1):
                            term = col[i6 + RADIUS + k] + col[i6 + RADIUS - k]
                            term = term + (cur[r, y0 + k : y0 + k + 8, :] + cur[r, y0 - k : y0 - k + 8, :])
                            acc = acc + (-0.5 * COEF[k]) * term
                        new[r, y0 : y0 + 8, :] = scale * acc + new[r, y0 : y0 + 8, :]

                if send is not False:

                    @when(send)
                    def _():
                        loop(48, lambda n: start(*out_args(0, blk * 8 + n // 6, n % 6)))

            loop(4, block)
            halo.wait_send()

        def two_steps(i):
            step(2 * i + 1, 0, buf0, buf1, False)

            @when(i < 4)
            def _():
                @when(i == 3)
                def _():
                    pl.semaphore_wait(mates, 7)

                step(2 * i + 2, 1, buf1, buf0, i == 3)

        loop(5, two_steps)
        gone(0)
        loop(192, lambda n: start(*out_args(1, n // 6, n % 6)))

    def r1_args(what, m):
        axes = {"orb": m % 8, "dom": (m // 8) * 32 + z * 2 + what}
        here = (tile == m) & (c == what)
        return here, gram.at[what, m], r1.at[meet_row * 4 + y_lo * 2 + c], r1_send.at[what, m], r1_recv, axes

    def r2_args(b):
        return b == z, mine.at[0], r2.at[z], r2_send.at[b], r2_recv, {"dom": y_lo * 32 + b * 2 + c}

    def r3_args(n):
        b, y, core = n // 4, (n // 2) % 2, n % 2
        here = (b == o) & (y == y_lo) & (core == c)
        axes = {"orb": b, "dom": y * 32 + z * 2 + core}
        return here, mine.at[1], full.at[c, tile], r3_send.at[n], full_recv.at[c], axes

    def meet_sums(what):
        @when(meets)
        def _():
            landed(every.at[what], m_recv.at[what])
            acc = jnp.zeros((NORB, NORB), F32)
            for s in range(8):
                acc = acc + lax.dot_general(
                    every[0, :, s, :], every[what, :, s, :], (((1,), (1,)), ((), ())),
                    precision=HI, preferred_element_type=F32,
                )
            for m in range(12):
                gram[what, m] = jnp.zeros((8, 128), F32)
                gram[what, m, :, 0:NORB] = acc[8 * m : 8 * m + 8, :]
            loop(12, lambda m: start(*r1_args(what, m)))

    def plane_sum(what):
        @when(owns & (c == what))
        def _():
            landed(r1, r1_recv)
            parts = [r1[b] for b in range(24)]
            while len(parts) > 1:
                parts = [sum(parts[i + 1 : i + 2], parts[i]) for i in range(0, len(parts), 2)]
            mine[0] = parts[0]
            loop(16, lambda b: start(*r2_args(b)))

    def whole_sum(what):
        @when(owns & (c == what))
        def _():
            landed(r2, r2_recv)
            parts = [r2[b] for b in range(16)]
            while len(parts) > 1:
                parts = [parts[i] + parts[i + 1] for i in range(0, len(parts), 2)]
            mine[1] = parts[0] * (1.0 / CELLS)
            loop(32, lambda n: start(*r3_args(n)))

    meet_sums(0)
    plane_sum(0)
    meet_sums(1)
    whole_sum(0)
    plane_sum(1)
    landed(full.at[0], full_recv.at[0])
    inverse = inverse_factor(full[0].reshape(NORB, 128), PAUSE, lambda: whole_sum(1))[:, :NORB]

    def o_args(b):
        dst = out_ref.at[:, 0, meet_row]
        return b == o, rot.at[pl.ds(b * 12, 12)], dst, o_send.at[b], o_recv, {"orb": b}

    @when(meets)
    def _():
        for s in range(8):
            rot[:, s, :] = jnp.dot(inverse, every[0, :, s, :], precision=HI, preferred_element_type=F32)
        loop(8, lambda b: start(*o_args(b)))

    loop(12, lambda j: left(*in_args(j)))

    @when(o < 6)
    def _():
        loop(12, lambda j: left(*pot_args(j)))

    @when(active)
    def _():
        @when(o < 6)
        def _():
            loop(32, lambda n: left(*share_args(n)))

        gone(1)

    for what in range(2):

        @when(meets)
        def _():
            loop(12, lambda m: left(*r1_args(what, m)))

    landed(full.at[1], full_recv.at[1])
    projected = full[1].reshape(NORB, 128)[:, :NORB]
    half = jnp.dot(inverse, projected, precision=HI, preferred_element_type=F32)
    sub[...] = lax.dot_general(
        half, inverse, (((1,), (1,)), ((), ())), precision=HI, preferred_element_type=F32
    )
    give = pltpu.make_async_copy(sub, sub_ref, sub_sem)
    give.start()

    @when(owns)
    def _():
        loop(16, lambda b: left(*r2_args(b)))
        loop(32, lambda n: left(*r3_args(n)))

    @when(meets)
    def _():
        loop(8, lambda b: left(*o_args(b)))

    landed(out_ref, o_recv)
    give.wait()


def local(orbitals, potential):
    anyspace = pl.BlockSpec(memory_space=pl.ANY)
    dma = pltpu.SemaphoreType.DMA
    return pl.pallas_call(
        kernel,
        out_shape=(
            jax.ShapeDtypeStruct(orbitals.shape, F32),
            jax.ShapeDtypeStruct((NORB, NORB), F32),
        ),
        in_specs=[anyspace, anyspace],
        out_specs=(anyspace, anyspace),
        scratch_shapes=[
            pltpu.VMEM((EXT_ROWS, EXT_COLS, 128), F32),
            pltpu.VMEM((EXT_ROWS, EXT_COLS, 128), F32),
            pltpu.VMEM((4, 6, 64, 128), F32),
            pltpu.VMEM((256, 384), jnp.bfloat16),
            pltpu.SMEM((32,), F32),
            pltpu.VMEM((2, NORB, 8, 128), F32),
            pltpu.VMEM((2, 12, 8, 128), F32),
            pltpu.VMEM((24, 8, 128), F32),
            pltpu.VMEM((16, 8, 128), F32),
            pltpu.VMEM((2, 8, 128), F32),
            pltpu.VMEM((2, 12, 8, 128), F32),
            pltpu.VMEM((NORB, 8, 128), F32),
            pltpu.VMEM((NORB, NORB), F32),
            dma((12,)), dma, dma((12,)), dma((4,)), dma((32,)), dma((6,)), dma((2,)), dma((2,)),
            dma((2, 32)), dma((2,)), pltpu.SemaphoreType.REGULAR,
            dma((2, 12)), dma, dma((16,)), dma, dma((32,)), dma((2,)), dma((8,)), dma, dma,
        ],
        compiler_params=pltpu.CompilerParams(
            collective_id=0, has_side_effects=True, vmem_limit_bytes=60 * 2**20
        ),
        name="filter_and_rotate",
    )(orbitals, potential)


def solution(mesh):
    return jax.shard_map(
        local,
        mesh=mesh,
        in_specs=(P("orb", "dom", None, None, None), P("dom", None, None, None)),
        out_specs=(P("orb", "dom", None, None, None), P()),
        check_vma=False,
    )
```

```python
import jax
import jax.numpy as jnp
from jax import lax
from jax.experimental import pallas as pl
from jax.experimental.pallas import tpu as pltpu
from jax.sharding import PartitionSpec as P

MESH = pl.DeviceIdType.MESH
HI = lax.Precision.HIGHEST
F32 = jnp.float32

NORB = 96
DEGREE = 8
RADIUS = 6
CELLS = 48 * 64 * 128

COEF = (
    -5369.0 / 1800.0,
    12.0 / 7.0,
    -15.0 / 56.0,
    10.0 / 189.0,
    -1.0 / 112.0,
    2.0 / 1925.0,
    -1.0 / 16632.0,
)
E_HALF = 6.0
CENTER = 8.0
A_LOW = 0.0

ROWS = 24
EXT_ROWS = ROWS + 2 * RADIUS
EXT_COLS = 80


def step_scalars():
    rows = [(0.0, 0.0, 0.0)]
    sigma = sigma_one = E_HALF / (A_LOW - CENTER)
    rows.append((sigma_one / E_HALF, CENTER, 0.0))
    for _ in range(2, DEGREE + 1):
        sigma_next = 1.0 / (2.0 / sigma_one - sigma)
        rows.append((2.0 * sigma_next / E_HALF, CENTER, sigma * sigma_next))
        sigma = sigma_next
    rows.append((1.0, 0.0, 0.0))
    return [(scale, center + 1.5 * COEF[0], past) for scale, center, past in rows]


def holder(j, c):
    y_lo, slot = j % 2, j // 2
    return y_lo * 32 + ((slot * 8) // 3 + y_lo) * 2 + c


def copy_to(src, dst, send, recv, axes):
    return pltpu.make_async_remote_copy(
        src_ref=src, dst_ref=dst, send_sem=send, recv_sem=recv, device_id=axes, device_id_type=MESH
    )


def landed(ref, sem):
    pltpu.make_async_copy(ref, ref, sem).wait()


def loop(n, body):
    lax.fori_loop(0, n, lambda i, carry: (body(i), carry)[1], 0)


def when(cond):
    return pl.when(cond)


def over_lanes(tile, j):
    return jnp.broadcast_to(tile[:, j : j + 1], (8, 128))


def over_rows(tile, r):
    return jnp.broadcast_to(tile[r : r + 1, :], (8, 128))


def inverse_factor(matrix):
    wide = 4
    sub = lax.broadcasted_iota(jnp.int32, (8, 128), 0)
    lane = lax.broadcasted_iota(jnp.int32, (8, 128), 1)
    tiles = NORB // 8
    st = [matrix[8 * t : 8 * t + 8, :] for t in range(tiles)]
    et = [jnp.where(lane == sub + 8 * t, 1.0, 0.0).astype(F32) for t in range(tiles)]
    for j in range(0, NORB, wide):
        t0, r = divmod(j, 8)
        cols = [[over_lanes(st[t], j + k) for k in range(wide)] for t in range(t0, tiles)]
        a = {(k, q): over_rows(cols[0][q], r + k) for k in range(wide) for q in range(k + 1)}
        inv, low = [], {}
        for p in range(wide):
            inv.append(1.0 / a[p, p])
            for k in range(p + 1, wide):
                low[k, p] = a[k, p] * inv[p]
            for k in range(p + 1, wide):
                for q in range(p + 1, k + 1):
                    a[k, q] = a[k, q] - low[k, p] * a[q, p]

        def forward(rows):
            done = []
            for k, row in enumerate(rows):
                for p in range(k):
                    row = row - low[k, p] * done[p]
                done.append(row)
            return done

        srow = forward([over_rows(st[t0], r + k) for k in range(wide)])
        erow = forward([over_rows(et[t0], r + k) for k in range(wide)])
        sdiv = [row * i for row, i in zip(srow, inv)]
        ediv = [row * i for row, i in zip(erow, inv)]
        for t in range(t0, tiles):
            if t == t0 and r + wide == 8:
                continue
            mult = []
            for k in range(wide):
                col = cols[t - t0][k]
                for p in range(k):
                    col = col - mult[p] * low[k, p]
                mult.append(col)
            if t == t0:
                mult = [jnp.where(sub >= r + wide, col, 0.0) for col in mult]
            for k in range(wide):
                st[t] = st[t] - mult[k] * sdiv[k]
                et[t] = et[t] - mult[k] * ediv[k]
        for k in range(wide):
            et[t0] = jnp.where(sub == r + k, erow[k] * lax.rsqrt(a[k, k]), et[t0])
    return jnp.concatenate(et, axis=0)


def kernel(
    orb_ref, pot_ref, out_ref, sub_ref,
    buf0, buf1, potb, w, scal, every, gram, r1, r2, mine, full, rot, sub,
    in_send, in_recv, p_send, p_recv, g_send, g_recv, h_send, h_recv, m_send, m_recv, mates,
    r1_send, r1_recv, r2_send, r2_recv, r3_send, full_recv, o_send, o_recv, sub_sem,
):
    d, o = lax.axis_index("dom"), lax.axis_index("orb")
    y_lo, z, c = d // 32, (d // 2) % 16, d % 2
    prow, pcol = d // 8, d % 8
    off = jnp.maximum(z - y_lo, 0)
    slot = (off * 3 + 2) // 8
    active = (z >= y_lo) & (slot < 6) & ((slot * 8) // 3 == off)
    orbital = slot * 2 + y_lo
    selfpair = active & (c == y_lo)
    meet_row = (o + 16 - z) % 8
    meets = meet_row < 6
    tile = y_lo * 8 + o
    owns = tile < 12

    def far_pencil(i):
        return (2 * z + 17 + jnp.where(i % 2 == 0, 32 - i // 2, (i + 1) // 2)) % 32

    barrier = pltpu.get_barrier_semaphore()

    def greet(cond, axes):
        @when(cond)
        def _():
            pl.semaphore_signal(barrier, inc=1, device_id=axes, device_id_type=MESH)

    def start(here, src, dst, send, recv, axes):
        @when(here)
        def _():
            pltpu.make_async_copy(src, dst, recv).start()

        @when(jnp.logical_not(here))
        def _():
            copy_to(src, dst, send, recv, axes).start()

    def left(here, src, dst, send, recv, axes):
        @when(jnp.logical_not(here))
        def _():
            copy_to(src, dst, send, recv, axes).wait_send()

    @when(active)
    def _():
        def source(i):
            m = c * 32 + far_pencil(i)
            greet(m != d, {"dom": m})

        loop(32, source)

    loop(8, lambda b: greet(b != o, {"orb": b}))

    partner = {"dom": d + 1 - 2 * c}

    @when(active)
    def _():
        margin, side = jnp.zeros((EXT_COLS, 128), F32), jnp.zeros((8, 128), F32)

        def clear(i):
            buf1[i] = margin
            buf0[i, 0:8, :] = side
            buf0[i, 72:80, :] = side

        loop(EXT_ROWS, clear)

        def clear_rows(i):
            buf0[i] = margin
            buf0[i + EXT_ROWS - RADIUS] = margin

        loop(RADIUS, clear_rows)
        gap = jnp.abs(
            lax.broadcasted_iota(jnp.int32, (128, 128), 0) - lax.broadcasted_iota(jnp.int32, (128, 128), 1)
        )
        weights = jnp.zeros((128, 128), F32)
        for k in range(1, RADIUS + 1):
            weights = jnp.where(gap == k, -0.5 * COEF[k], weights)
        high = weights.astype(jnp.bfloat16)
        rest = weights - high.astype(F32)
        middle = rest.astype(jnp.bfloat16)
        low = (rest - middle.astype(F32)).astype(jnp.bfloat16)
        for i, row in enumerate(((high, middle, high), (high, middle, low))):
            for n, part in enumerate(row):
                w[128 * i : 128 * i + 128, 128 * n : 128 * n + 128] = part
        for s, row in enumerate(step_scalars()):
            for i, value in enumerate(row):
                scal[3 * s + i] = jnp.float32(value)
        greet(active, partner)

    pl.semaphore_wait(barrier, 19 + active.astype(jnp.int32) - selfpair.astype(jnp.int32))

    far = (((z + 8) % 16) * 3) // 4
    col0 = pl.multiple_of(pcol * 8, 8)

    def far_first(i):
        return (far + 12 + jnp.where(i % 2 == 0, -(i // 2), (i + 1) // 2)) % 12

    def pot_args(j):
        t = holder(j, y_lo)
        return t == d, pot_ref.at[0, o], potb.at[prow % 4, o, pl.ds(col0, 8)], p_send.at[j], p_recv.at[prow % 4], {"dom": t}

    def in_args(j):
        t = holder(j, y_lo)
        dst = buf0.at[pl.ds(RADIUS + (prow % 4) * 6, 6), pl.ds(pl.multiple_of(8 + pcol * 8, 8), 8)]
        return t == d, orb_ref.at[j, 0], dst, in_send.at[j], in_recv, {"dom": t}

    @when(o < 6)
    def _():
        loop(12, lambda i: start(*pot_args(far_first(i))))

    def send_in():
        loop(12, lambda i: start(*in_args(far_first(i))))

    @when(jnp.logical_not(active))
    def _():
        send_in()


    def share_args(n):
        q, b = n // 8, n % 8
        return b == o, potb.at[q, o], potb.at[q, o], g_send.at[n], g_recv.at[o], {"orb": b}

    def out_args(what, m, r):
        src = (buf0, buf1)[what].at[RADIUS + (m // 8) * 6 + r, pl.ds(pl.multiple_of(8 + (m % 8) * 8, 8), 8)]
        t = c * 32 + m
        b = (r + m // 2) % 8
        axes = {"orb": b, "dom": t}
        return (t == d) & (b == o), src, every.at[what, o * 12 + orbital], m_send.at[what, m], m_recv.at[what], axes

    def gone(what, first, count):
        def one(i):
            m = far_pencil(first + i)
            alone = (c * 32 + m == d) & meets

            @when(alone)
            def _():
                landed(every.at[what, pl.ds(0, 5)], m_send.at[what, m])

            @when(jnp.logical_not(alone))
            def _():
                landed(every.at[what, pl.ds(0, 6)], m_send.at[what, m])

        loop(count, one)

    @when(active)
    def _():
        @when(o < 6)
        def _():
            def share(i):
                q = (z // 4 + jnp.where(i == 2, 3, jnp.where(i == 3, 2, i))) % 4
                landed(potb.at[q, 0], p_recv.at[q])

                def one(b):
                    here, src, dst, send, recv, axes = share_args(q * 8 + b)

                    @when(jnp.logical_not(here))
                    def _():
                        copy_to(src, dst, send, recv, axes).start()

                loop(8, one)

            loop(4, share)

        send_in()

        def shared(r):
            @when(r != o)
            def _():
                landed(potb.at[:, 0], g_recv.at[r])

        loop(6, shared)
        landed(buf0.at[pl.ds(RADIUS, ROWS), pl.ds(8, 64)], in_recv)

        def tell(b):
            @when(b != o)
            def _():
                pl.semaphore_signal(mates, inc=1, device_id={"orb": b}, device_id_type=MESH)

        loop(8, tell)

        def step(s, what, cur, new):
            halo = copy_to(
                cur.at[pl.ds(24 - 18 * c, 6), pl.ds(8, 64)],
                cur.at[pl.ds(30 * c, 6), pl.ds(8, 64)],
                h_send.at[what], h_recv.at[what], partner,
            )
            halo.start()
            scale, shift, past = scal[3 * s], scal[3 * s + 1], scal[3 * s + 2]
            x = cur[RADIUS : RADIUS + ROWS, 8:72, :].reshape(ROWS * 64, 128)
            high = x.astype(jnp.bfloat16)
            rest = x - high.astype(F32)
            middle = rest.astype(jnp.bfloat16)
            low = (rest - middle.astype(F32)).astype(jnp.bfloat16)
            most = jnp.dot(jnp.concatenate([high, middle], axis=1), w[:, :256], preferred_element_type=F32)
            small = jnp.dot(jnp.concatenate([low, high], axis=1), w[:, 256:], preferred_element_type=F32)
            along = ((most[:, 128:] + small) + most[:, :128]).reshape(ROWS, 64, 128)
            new[RADIUS : RADIUS + ROWS, 8:72, :] = scale * along - past * new[RADIUS : RADIUS + ROWS, 8:72, :]

            def block(i):
                @when(i == 3)
                def _():
                    halo.wait_recv()

                blk = jnp.where(c == 0, i, 3 - i)
                r0 = RADIUS + blk * 6
                for yt in range(8):
                    y0 = 8 + 8 * yt
                    col = [cur[r0 - RADIUS + m, y0 : y0 + 8, :] for m in range(18)]
                    for i6 in range(6):
                        r = r0 + i6
                        mid = col[i6 + RADIUS]
                        acc = (potb[blk, i6, y0 - 8 : y0, :] - shift) * mid
                        for k in range(1, RADIUS + 1):
                            term = col[i6 + RADIUS + k] + col[i6 + RADIUS - k]
                            term = term + (cur[r, y0 + k : y0 + k + 8, :] + cur[r, y0 - k : y0 - k + 8, :])
                            acc = acc + (-0.5 * COEF[k]) * term
                        new[r, y0 : y0 + 8, :] = scale * acc + new[r, y0 : y0 + 8, :]

            loop(4, block)
            halo.wait_send()

        def two_steps(i):
            step(2 * i + 1, 0, buf0, buf1)

            @when(i < 4)
            def _():
                step(2 * i + 2, 1, buf1, buf0)

            @when(i == 3)
            def _():
                pl.semaphore_wait(mates, 7)
                loop(192, lambda n: start(*out_args(0, far_pencil(n // 6), n % 6)))

        loop(5, two_steps)
        gone(0, 0, 28)
        loop(192, lambda n: start(*out_args(1, far_pencil(n // 6), n % 6)))

    def r1_args(what, m):
        axes = {"orb": m % 8, "dom": (m // 8) * 32 + z * 2 + what}
        here = (tile == m) & (c == what)
        return here, gram.at[what, m], r1.at[meet_row * 4 + y_lo * 2 + c], r1_send.at[what, m], r1_recv, axes

    def r2_args(b):
        return b == z, mine.at[0], r2.at[z], r2_send.at[b], r2_recv, {"dom": y_lo * 32 + b * 2 + c}

    def r3_args(n):
        b, y, core = n // 4, (n // 2) % 2, n % 2
        here = (b == o) & (y == y_lo) & (core == c)
        axes = {"orb": b, "dom": y * 32 + z * 2 + core}
        return here, mine.at[1], full.at[c, tile], r3_send.at[n], full_recv.at[c], axes

    def meet_sums(what):
        @when(meets)
        def _():
            landed(every.at[what], m_recv.at[what])
            acc = jnp.zeros((NORB, NORB), F32)
            for s in range(8):
                acc = acc + lax.dot_general(
                    every[0, :, s, :], every[what, :, s, :], (((1,), (1,)), ((), ())),
                    precision=HI, preferred_element_type=F32,
                )
            for m in range(12):
                gram[what, m] = jnp.zeros((8, 128), F32)
                gram[what, m, :, 0:NORB] = acc[8 * m : 8 * m + 8, :]
            loop(12, lambda m: start(*r1_args(what, m)))

    def plane_sum(what):
        @when(owns & (c == what))
        def _():
            landed(r1, r1_recv)
            parts = [r1[b] for b in range(24)]
            while len(parts) > 1:
                parts = [sum(parts[i + 1 : i + 2], parts[i]) for i in range(0, len(parts), 2)]
            mine[0] = parts[0]
            loop(16, lambda b: start(*r2_args(b)))

    def whole_sum(what):
        @when(owns & (c == what))
        def _():
            landed(r2, r2_recv)
            parts = [r2[b] for b in range(16)]
            while len(parts) > 1:
                parts = [parts[i] + parts[i + 1] for i in range(0, len(parts), 2)]
            mine[1] = parts[0] * (1.0 / CELLS)
            loop(32, lambda n: start(*r3_args(n)))

    meet_sums(0)
    plane_sum(0)
    meet_sums(1)
    whole_sum(0)
    plane_sum(1)
    landed(full.at[0], full_recv.at[0])
    inverse = inverse_factor(full[0].reshape(NORB, 128))[:, :NORB]

    def o_args(b):
        dst = out_ref.at[:, 0, meet_row]
        return b == o, rot.at[pl.ds(b * 12, 12)], dst, o_send.at[b], o_recv, {"orb": b}

    @when(meets)
    def _():
        for s in range(8):
            rot[:, s, :] = jnp.dot(inverse, every[0, :, s, :], precision=HI, preferred_element_type=F32)
        loop(8, lambda b: start(*o_args(b)))

    whole_sum(1)

    loop(12, lambda j: left(*in_args(j)))

    @when(o < 6)
    def _():
        loop(12, lambda j: left(*pot_args(j)))

    @when(active)
    def _():
        @when(o < 6)
        def _():
            loop(32, lambda n: left(*share_args(n)))

        gone(0, 28, 4)
        gone(1, 0, 32)

    for what in range(2):

        @when(meets)
        def _():
            loop(12, lambda m: left(*r1_args(what, m)))

    landed(full.at[1], full_recv.at[1])
    projected = full[1].reshape(NORB, 128)[:, :NORB]
    half = jnp.dot(inverse, projected, precision=HI, preferred_element_type=F32)
    sub[...] = lax.dot_general(
        half, inverse, (((1,), (1,)), ((), ())), precision=HI, preferred_element_type=F32
    )
    give = pltpu.make_async_copy(sub, sub_ref, sub_sem)
    give.start()

    @when(owns)
    def _():
        loop(16, lambda b: left(*r2_args(b)))
        loop(32, lambda n: left(*r3_args(n)))

    @when(meets)
    def _():
        loop(8, lambda b: left(*o_args(b)))

    landed(out_ref, o_recv)
    give.wait()


def local(orbitals, potential):
    anyspace = pl.BlockSpec(memory_space=pl.ANY)
    dma = pltpu.SemaphoreType.DMA
    return pl.pallas_call(
        kernel,
        out_shape=(
            jax.ShapeDtypeStruct(orbitals.shape, F32),
            jax.ShapeDtypeStruct((NORB, NORB), F32),
        ),
        in_specs=[anyspace, anyspace],
        out_specs=(anyspace, anyspace),
        scratch_shapes=[
            pltpu.VMEM((EXT_ROWS, EXT_COLS, 128), F32),
            pltpu.VMEM((EXT_ROWS, EXT_COLS, 128), F32),
            pltpu.VMEM((4, 6, 64, 128), F32),
            pltpu.VMEM((256, 384), jnp.bfloat16),
            pltpu.SMEM((32,), F32),
            pltpu.VMEM((2, NORB, 8, 128), F32),
            pltpu.VMEM((2, 12, 8, 128), F32),
            pltpu.VMEM((24, 8, 128), F32),
            pltpu.VMEM((16, 8, 128), F32),
            pltpu.VMEM((2, 8, 128), F32),
            pltpu.VMEM((2, 12, 8, 128), F32),
            pltpu.VMEM((NORB, 8, 128), F32),
            pltpu.VMEM((NORB, NORB), F32),
            dma((12,)), dma, dma((12,)), dma((4,)), dma((32,)), dma((6,)), dma((2,)), dma((2,)),
            dma((2, 32)), dma((2,)), pltpu.SemaphoreType.REGULAR,
            dma((2, 12)), dma, dma((16,)), dma, dma((32,)), dma((2,)), dma((8,)), dma, dma,
        ],
        compiler_params=pltpu.CompilerParams(
            collective_id=0, has_side_effects=True, vmem_limit_bytes=60 * 2**20
        ),
        name="filter_and_rotate",
    )(orbitals, potential)


def solution(mesh):
    return jax.shard_map(
        local,
        mesh=mesh,
        in_specs=(P("orb", "dom", None, None, None), P("dom", None, None, None)),
        out_specs=(P("orb", "dom", None, None, None), P()),
        check_vma=False,
    )
```

```python
import jax
import jax.numpy as jnp
from jax import lax
from jax.experimental import pallas as pl
from jax.experimental.pallas import tpu as pltpu
from jax.sharding import PartitionSpec as P

MESH = pl.DeviceIdType.MESH
HI = lax.Precision.HIGHEST
F32 = jnp.float32

NORB = 96
DEGREE = 8
RADIUS = 6
CELLS = 48 * 64 * 128

COEF = (
    -5369.0 / 1800.0,
    12.0 / 7.0,
    -15.0 / 56.0,
    10.0 / 189.0,
    -1.0 / 112.0,
    2.0 / 1925.0,
    -1.0 / 16632.0,
)
E_HALF = 6.0
CENTER = 8.0
A_LOW = 0.0

ROWS = 24
EXT_ROWS = ROWS + 2 * RADIUS
EXT_COLS = 80


def step_scalars():
    rows = [(0.0, 0.0, 0.0)]
    sigma = sigma_one = E_HALF / (A_LOW - CENTER)
    rows.append((sigma_one / E_HALF, CENTER, 0.0))
    for _ in range(2, DEGREE + 1):
        sigma_next = 1.0 / (2.0 / sigma_one - sigma)
        rows.append((2.0 * sigma_next / E_HALF, CENTER, sigma * sigma_next))
        sigma = sigma_next
    rows.append((1.0, 0.0, 0.0))
    return [(scale, center + 1.5 * COEF[0], past) for scale, center, past in rows]


def holder(j, c):
    y_lo, slot = j % 2, j // 2
    return y_lo * 32 + ((slot * 8) // 3 + y_lo) * 2 + c


def copy_to(src, dst, send, recv, axes):
    return pltpu.make_async_remote_copy(
        src_ref=src, dst_ref=dst, send_sem=send, recv_sem=recv, device_id=axes, device_id_type=MESH
    )


def landed(ref, sem):
    pltpu.make_async_copy(ref, ref, sem).wait()


def loop(n, body):
    lax.fori_loop(0, n, lambda i, carry: (body(i), carry)[1], 0)


def when(cond):
    return pl.when(cond)


def over_lanes(tile, j):
    return jnp.broadcast_to(tile[:, j : j + 1], (8, 128))


def over_rows(tile, r):
    return jnp.broadcast_to(tile[r : r + 1, :], (8, 128))


def inverse_factor(matrix):
    wide = 4
    sub = lax.broadcasted_iota(jnp.int32, (8, 128), 0)
    lane = lax.broadcasted_iota(jnp.int32, (8, 128), 1)
    tiles = NORB // 8
    st = [matrix[8 * t : 8 * t + 8, :] for t in range(tiles)]
    et = [jnp.where(lane == sub + 8 * t, 1.0, 0.0).astype(F32) for t in range(tiles)]
    for j in range(0, NORB, wide):
        t0, r = divmod(j, 8)
        cols = [[over_lanes(st[t], j + k) for k in range(wide)] for t in range(t0, tiles)]
        a = {(k, q): over_rows(cols[0][q], r + k) for k in range(wide) for q in range(k + 1)}
        inv, low = [], {}
        for p in range(wide):
            inv.append(1.0 / a[p, p])
            for k in range(p + 1, wide):
                low[k, p] = a[k, p] * inv[p]
            for k in range(p + 1, wide):
                for q in range(p + 1, k + 1):
                    a[k, q] = a[k, q] - low[k, p] * a[q, p]

        def forward(rows):
            done = []
            for k, row in enumerate(rows):
                for p in range(k):
                    row = row - low[k, p] * done[p]
                done.append(row)
            return done

        srow = forward([over_rows(st[t0], r + k) for k in range(wide)])
        erow = forward([over_rows(et[t0], r + k) for k in range(wide)])
        sdiv = [row * i for row, i in zip(srow, inv)]
        ediv = [row * i for row, i in zip(erow, inv)]
        for t in range(t0, tiles):
            if t == t0 and r + wide == 8:
                continue
            mult = []
            for k in range(wide):
                col = cols[t - t0][k]
                for p in range(k):
                    col = col - mult[p] * low[k, p]
                mult.append(col)
            if t == t0:
                mult = [jnp.where(sub >= r + wide, col, 0.0) for col in mult]
            for k in range(wide):
                st[t] = st[t] - mult[k] * sdiv[k]
                et[t] = et[t] - mult[k] * ediv[k]
        for k in range(wide):
            et[t0] = jnp.where(sub == r + k, erow[k] * lax.rsqrt(a[k, k]), et[t0])
    return jnp.concatenate(et, axis=0)


def kernel(
    orb_ref, pot_ref, out_ref, sub_ref,
    buf0, buf1, potb, w, scal, every, gram, r1, r2, mine, full, rot, inv, sub,
    in_send, in_recv, p_send, p_recv, g_send, g_recv, h_send, h_recv, m_send, m_recv, mates,
    r1_send, r1_recv, r2_send, r2_recv, r3_send, full_recv, o_send, o_recv, sub_sem,
):
    d, o = lax.axis_index("dom"), lax.axis_index("orb")
    y_lo, z, c = d // 32, (d // 2) % 16, d % 2
    prow, pcol = d // 8, d % 8
    off = jnp.maximum(z - y_lo, 0)
    slot = (off * 3 + 2) // 8
    active = (z >= y_lo) & (slot < 6) & ((slot * 8) // 3 == off)
    orbital = slot * 2 + y_lo
    selfpair = active & (c == y_lo)
    meet_row = (o + 16 - z) % 8
    meets = meet_row < 6
    tile = y_lo * 8 + o
    owns = tile < 12

    def far_pencil(i):
        return (2 * z + 17 + jnp.where(i % 2 == 0, 32 - i // 2, (i + 1) // 2)) % 32

    def far_group(i):
        across = (i < 3) | (i == 4)
        along = jnp.where((i == 0) | (i == 3), 2, jnp.where((i == 1) | (i == 5), 1, jnp.where((i == 2) | (i == 6), 3, 0)))
        return ((o // 4 + across.astype(jnp.int32)) % 2) * 4 + (o % 4 + along) % 4

    barrier = pltpu.get_barrier_semaphore()

    def greet(cond, axes):
        @when(cond)
        def _():
            pl.semaphore_signal(barrier, inc=1, device_id=axes, device_id_type=MESH)

    def start(here, src, dst, send, recv, axes):
        @when(here)
        def _():
            pltpu.make_async_copy(src, dst, recv).start()

        @when(jnp.logical_not(here))
        def _():
            copy_to(src, dst, send, recv, axes).start()

    def left(here, src, dst, send, recv, axes):
        @when(jnp.logical_not(here))
        def _():
            copy_to(src, dst, send, recv, axes).wait_send()

    @when(active)
    def _():
        def source(i):
            m = c * 32 + far_pencil(i)
            greet(m != d, {"dom": m})

        loop(32, source)

    loop(8, lambda b: greet(b != o, {"orb": b}))

    partner = {"dom": d + 1 - 2 * c}

    @when(active)
    def _():
        margin, side = jnp.zeros((EXT_COLS, 128), F32), jnp.zeros((8, 128), F32)

        def clear(i):
            buf1[i] = margin
            buf0[i, 0:8, :] = side
            buf0[i, 72:80, :] = side

        loop(EXT_ROWS, clear)

        def clear_rows(i):
            buf0[i] = margin
            buf0[i + EXT_ROWS - RADIUS] = margin

        loop(RADIUS, clear_rows)
        gap = jnp.abs(
            lax.broadcasted_iota(jnp.int32, (128, 128), 0) - lax.broadcasted_iota(jnp.int32, (128, 128), 1)
        )
        weights = jnp.zeros((128, 128), F32)
        for k in range(1, RADIUS + 1):
            weights = jnp.where(gap == k, -0.5 * COEF[k], weights)
        high = weights.astype(jnp.bfloat16)
        rest = weights - high.astype(F32)
        middle = rest.astype(jnp.bfloat16)
        low = (rest - middle.astype(F32)).astype(jnp.bfloat16)
        for i, row in enumerate(((high, middle, high), (high, middle, low))):
            for n, part in enumerate(row):
                w[128 * i : 128 * i + 128, 128 * n : 128 * n + 128] = part
        for s, row in enumerate(step_scalars()):
            for i, value in enumerate(row):
                scal[3 * s + i] = jnp.float32(value)
        greet(active, partner)

    pl.semaphore_wait(barrier, 19 + active.astype(jnp.int32) - selfpair.astype(jnp.int32))

    far = (((z + 8) % 16) * 3) // 4
    col0 = pl.multiple_of(pcol * 8, 8)

    def far_first(i):
        return (far + 12 + jnp.where(i % 2 == 0, -(i // 2), (i + 1) // 2)) % 12

    def pot_args(j):
        t = holder(j, y_lo)
        return t == d, pot_ref.at[0, o], potb.at[prow % 4, o, pl.ds(col0, 8)], p_send.at[j], p_recv.at[prow % 4], {"dom": t}

    def in_args(j):
        t = holder(j, y_lo)
        dst = buf0.at[pl.ds(RADIUS + (prow % 4) * 6, 6), pl.ds(pl.multiple_of(8 + pcol * 8, 8), 8)]
        return t == d, orb_ref.at[j, 0], dst, in_send.at[j], in_recv, {"dom": t}

    @when(o < 6)
    def _():
        loop(12, lambda i: start(*pot_args(far_first(i))))

    def send_in(first, count):
        loop(count, lambda i: start(*in_args(far_first(first + i))))

    @when(jnp.logical_not(active))
    def _():
        send_in(0, 12)


    def share_args(n):
        q, b = n // 8, n % 8
        return b == o, potb.at[q, o], potb.at[q, o], g_send.at[n], g_recv.at[o], {"orb": b}

    def out_args(what, m, r):
        src = (buf0, buf1)[what].at[RADIUS + (m // 8) * 6 + r, pl.ds(pl.multiple_of(8 + (m % 8) * 8, 8), 8)]
        t = c * 32 + m
        b = (r + m // 2) % 8
        axes = {"orb": b, "dom": t}
        return (t == d) & (b == o), src, every.at[what, o * 12 + orbital], m_send.at[what, m], m_recv.at[what], axes

    def gone(what, first, count):
        def one(i):
            m = far_pencil(first + i)
            alone = (c * 32 + m == d) & meets

            @when(alone)
            def _():
                landed(every.at[what, pl.ds(0, 5)], m_send.at[what, m])

            @when(jnp.logical_not(alone))
            def _():
                landed(every.at[what, pl.ds(0, 6)], m_send.at[what, m])

        loop(count, one)

    @when(active)
    def _():
        def share(first, count):
            def part(n):
                i = first + n
                q = (z // 4 + jnp.where(i == 2, 3, jnp.where(i == 3, 2, i))) % 4
                landed(potb.at[q, 0], p_recv.at[q])

                def one(b):
                    here, src, dst, send, recv, axes = share_args(q * 8 + far_group(b))

                    @when(jnp.logical_not(here))
                    def _():
                        copy_to(src, dst, send, recv, axes).start()

                loop(8, one)

            @when(o < 6)
            def _():
                loop(count, part)

        share(0, 2)
        send_in(0, 4)
        share(2, 1)
        send_in(4, 4)
        share(3, 1)
        send_in(8, 4)

        def shared(r):
            @when(r != o)
            def _():
                landed(potb.at[:, 0], g_recv.at[r])

        loop(6, shared)
        landed(buf0.at[pl.ds(RADIUS, ROWS), pl.ds(8, 64)], in_recv)

        def tell(b):
            @when(b != o)
            def _():
                pl.semaphore_signal(mates, inc=1, device_id={"orb": b}, device_id_type=MESH)

        loop(8, tell)

        def step(s, what, cur, new):
            halo = copy_to(
                cur.at[pl.ds(24 - 18 * c, 6), pl.ds(8, 64)],
                cur.at[pl.ds(30 * c, 6), pl.ds(8, 64)],
                h_send.at[what], h_recv.at[what], partner,
            )
            halo.start()
            scale, shift, past = scal[3 * s], scal[3 * s + 1], scal[3 * s + 2]
            x = cur[RADIUS : RADIUS + ROWS, 8:72, :].reshape(ROWS * 64, 128)
            high = x.astype(jnp.bfloat16)
            rest = x - high.astype(F32)
            middle = rest.astype(jnp.bfloat16)
            low = (rest - middle.astype(F32)).astype(jnp.bfloat16)
            most = jnp.dot(jnp.concatenate([high, middle], axis=1), w[:, :256], preferred_element_type=F32)
            small = jnp.dot(jnp.concatenate([low, high], axis=1), w[:, 256:], preferred_element_type=F32)
            along = ((most[:, 128:] + small) + most[:, :128]).reshape(ROWS, 64, 128)
            new[RADIUS : RADIUS + ROWS, 8:72, :] = scale * along - past * new[RADIUS : RADIUS + ROWS, 8:72, :]

            def block(i):
                @when(i == 3)
                def _():
                    halo.wait_recv()

                blk = jnp.where(c == 0, i, 3 - i)
                r0 = RADIUS + blk * 6
                for yt in range(8):
                    y0 = 8 + 8 * yt
                    col = [cur[r0 - RADIUS + m, y0 : y0 + 8, :] for m in range(18)]
                    for i6 in range(6):
                        r = r0 + i6
                        mid = col[i6 + RADIUS]
                        acc = (potb[blk, i6, y0 - 8 : y0, :] - shift) * mid
                        for k in range(1, RADIUS + 1):
                            term = col[i6 + RADIUS + k] + col[i6 + RADIUS - k]
                            term = term + (cur[r, y0 + k : y0 + k + 8, :] + cur[r, y0 - k : y0 - k + 8, :])
                            acc = acc + (-0.5 * COEF[k]) * term
                        new[r, y0 : y0 + 8, :] = scale * acc + new[r, y0 : y0 + 8, :]

            loop(4, block)
            halo.wait_send()

        def two_steps(i):
            step(2 * i + 1, 0, buf0, buf1)

            @when(i < 4)
            def _():
                step(2 * i + 2, 1, buf1, buf0)

            @when(i == 3)
            def _():
                pl.semaphore_wait(mates, 7)
                loop(192, lambda n: start(*out_args(0, far_pencil(n // 6), n % 6)))

        loop(5, two_steps)
        gone(0, 0, 28)
        loop(192, lambda n: start(*out_args(1, far_pencil(n // 6), n % 6)))

    def r1_args(what, m):
        axes = {"orb": m % 8, "dom": (m // 8) * 32 + z * 2 + what}
        here = (tile == m) & (c == what)
        return here, gram.at[what, m], r1.at[meet_row * 4 + y_lo * 2 + c], r1_send.at[what, m], r1_recv, axes

    def r2_args(b):
        return b == z, mine.at[0], r2.at[z], r2_send.at[b], r2_recv, {"dom": y_lo * 32 + b * 2 + c}

    def r3_args(n):
        b, y, core = n // 4, (n // 2) % 2, n % 2
        here = (b == o) & (y == y_lo) & (core == c)
        axes = {"orb": b, "dom": y * 32 + z * 2 + core}
        return here, mine.at[1], full.at[c, tile], r3_send.at[n], full_recv.at[c], axes

    def meet_sums(what):
        @when(meets)
        def _():
            landed(every.at[what], m_recv.at[what])
            acc = jnp.zeros((NORB, NORB), F32)
            for s in range(8):
                acc = acc + lax.dot_general(
                    every[0, :, s, :], every[what, :, s, :], (((1,), (1,)), ((), ())),
                    precision=HI, preferred_element_type=F32,
                )
            for m in range(12):
                gram[what, m] = jnp.zeros((8, 128), F32)
                gram[what, m, :, 0:NORB] = acc[8 * m : 8 * m + 8, :]
            loop(12, lambda m: start(*r1_args(what, m)))

    def plane_sum(what):
        @when(owns & (c == what))
        def _():
            landed(r1, r1_recv)
            parts = [r1[b] for b in range(24)]
            while len(parts) > 1:
                parts = [sum(parts[i + 1 : i + 2], parts[i]) for i in range(0, len(parts), 2)]
            mine[0] = parts[0]
            loop(16, lambda i: start(*r2_args((z + 8 + jnp.where(i % 2 == 0, 16 - i // 2, (i + 1) // 2)) % 16)))

    def whole_sum(what):
        @when(owns & (c == what))
        def _():
            landed(r2, r2_recv)
            parts = [r2[b] for b in range(16)]
            while len(parts) > 1:
                parts = [parts[i] + parts[i + 1] for i in range(0, len(parts), 2)]
            mine[1] = parts[0] * (1.0 / CELLS)
            loop(32, lambda n: start(*r3_args(far_group(n // 4) * 4 + n % 4)))

    meet_sums(0)
    plane_sum(0)
    meet_sums(1)
    whole_sum(0)
    plane_sum(1)
    landed(full.at[0], full_recv.at[0])
    inverse = inverse_factor(full[0].reshape(NORB, 128))[:, :NORB]

    def o_args(b):
        dst = out_ref.at[:, 0, meet_row]
        return b == o, rot.at[pl.ds(b * 12, 12)], dst, o_send.at[b], o_recv, {"orb": b}

    @when(meets)
    def _():
        inv[...] = inverse

        def rotate(i):
            half = (o // 4 + 1 + i) % 2
            rows = pl.ds(pl.multiple_of(half * 48, 8), 48)
            part = inv[rows, :]
            for s in range(8):
                rot[rows, s, :] = jnp.dot(part, every[0, :, s, :], precision=HI, preferred_element_type=F32)
            loop(4, lambda n: start(*o_args(half * 4 + (o % 4 + jnp.where(n == 0, 2, n + n // 3 - 1)) % 4)))

        loop(2, rotate)

    whole_sum(1)

    loop(12, lambda j: left(*in_args(j)))

    @when(o < 6)
    def _():
        loop(12, lambda j: left(*pot_args(j)))

    @when(active)
    def _():
        @when(o < 6)
        def _():
            loop(32, lambda n: left(*share_args(n)))

        gone(0, 28, 4)
        gone(1, 0, 32)

    for what in range(2):

        @when(meets)
        def _():
            loop(12, lambda m: left(*r1_args(what, m)))

    landed(full.at[1], full_recv.at[1])
    projected = full[1].reshape(NORB, 128)[:, :NORB]
    half = jnp.dot(inverse, projected, precision=HI, preferred_element_type=F32)
    sub[...] = lax.dot_general(
        half, inverse, (((1,), (1,)), ((), ())), precision=HI, preferred_element_type=F32
    )
    give = pltpu.make_async_copy(sub, sub_ref, sub_sem)
    give.start()

    @when(owns)
    def _():
        loop(16, lambda b: left(*r2_args(b)))
        loop(32, lambda n: left(*r3_args(n)))

    @when(meets)
    def _():
        loop(8, lambda b: left(*o_args(b)))

    landed(out_ref, o_recv)
    give.wait()


def local(orbitals, potential):
    anyspace = pl.BlockSpec(memory_space=pl.ANY)
    dma = pltpu.SemaphoreType.DMA
    return pl.pallas_call(
        kernel,
        out_shape=(
            jax.ShapeDtypeStruct(orbitals.shape, F32),
            jax.ShapeDtypeStruct((NORB, NORB), F32),
        ),
        in_specs=[anyspace, anyspace],
        out_specs=(anyspace, anyspace),
        scratch_shapes=[
            pltpu.VMEM((EXT_ROWS, EXT_COLS, 128), F32),
            pltpu.VMEM((EXT_ROWS, EXT_COLS, 128), F32),
            pltpu.VMEM((4, 6, 64, 128), F32),
            pltpu.VMEM((256, 384), jnp.bfloat16),
            pltpu.SMEM((32,), F32),
            pltpu.VMEM((2, NORB, 8, 128), F32),
            pltpu.VMEM((2, 12, 8, 128), F32),
            pltpu.VMEM((24, 8, 128), F32),
            pltpu.VMEM((16, 8, 128), F32),
            pltpu.VMEM((2, 8, 128), F32),
            pltpu.VMEM((2, 12, 8, 128), F32),
            pltpu.VMEM((NORB, 8, 128), F32),
            pltpu.VMEM((NORB, NORB), F32),
            pltpu.VMEM((NORB, NORB), F32),
            dma((12,)), dma, dma((12,)), dma((4,)), dma((32,)), dma((6,)), dma((2,)), dma((2,)),
            dma((2, 32)), dma((2,)), pltpu.SemaphoreType.REGULAR,
            dma((2, 12)), dma, dma((16,)), dma, dma((32,)), dma((2,)), dma((8,)), dma, dma,
        ],
        compiler_params=pltpu.CompilerParams(
            collective_id=0, has_side_effects=True, vmem_limit_bytes=60 * 2**20
        ),
        name="filter_and_rotate",
    )(orbitals, potential)


def solution(mesh):
    return jax.shard_map(
        local,
        mesh=mesh,
        in_specs=(P("orb", "dom", None, None, None), P("dom", None, None, None)),
        out_specs=(P("orb", "dom", None, None, None), P()),
        check_vma=False,
    )
```

```python
import jax
import jax.numpy as jnp
from jax import lax
from jax.experimental import pallas as pl
from jax.experimental.pallas import tpu as pltpu
from jax.sharding import PartitionSpec as P

MESH = pl.DeviceIdType.MESH
HI = lax.Precision.HIGHEST
F32 = jnp.float32

NORB = 96
DEGREE = 8
RADIUS = 6
CELLS = 48 * 64 * 128

COEF = (
    -5369.0 / 1800.0,
    12.0 / 7.0,
    -15.0 / 56.0,
    10.0 / 189.0,
    -1.0 / 112.0,
    2.0 / 1925.0,
    -1.0 / 16632.0,
)
E_HALF = 6.0
CENTER = 8.0
A_LOW = 0.0

ROWS = 24
EXT_ROWS = ROWS + 2 * RADIUS
EXT_COLS = 80


def step_scalars():
    rows = [(0.0, 0.0, 0.0)]
    sigma = sigma_one = E_HALF / (A_LOW - CENTER)
    rows.append((sigma_one / E_HALF, CENTER, 0.0))
    for _ in range(2, DEGREE + 1):
        sigma_next = 1.0 / (2.0 / sigma_one - sigma)
        rows.append((2.0 * sigma_next / E_HALF, CENTER, sigma * sigma_next))
        sigma = sigma_next
    rows.append((1.0, 0.0, 0.0))
    return [(scale, center + 1.5 * COEF[0], past) for scale, center, past in rows]


def holder(j, c):
    y_lo, slot = j % 2, j // 2
    return y_lo * 32 + ((slot * 8) // 3 + y_lo) * 2 + c


def copy_to(src, dst, send, recv, axes):
    return pltpu.make_async_remote_copy(
        src_ref=src, dst_ref=dst, send_sem=send, recv_sem=recv, device_id=axes, device_id_type=MESH
    )


def landed(ref, sem):
    pltpu.make_async_copy(ref, ref, sem).wait()


def loop(n, body):
    lax.fori_loop(0, n, lambda i, carry: (body(i), carry)[1], 0)


def when(cond):
    return pl.when(cond)


def over_lanes(tile, j):
    return jnp.broadcast_to(tile[:, j : j + 1], (8, 128))


def over_rows(tile, r):
    return jnp.broadcast_to(tile[r : r + 1, :], (8, 128))


def split(every, what):
    x = jnp.concatenate([every[what, :, s, :] for s in range(8)], axis=1)
    high = x.astype(jnp.bfloat16)
    rest = x - high.astype(F32)
    middle = rest.astype(jnp.bfloat16)
    return high, middle, (rest - middle.astype(F32)).astype(jnp.bfloat16)


def inverse_factor(matrix):
    wide = 4
    sub = lax.broadcasted_iota(jnp.int32, (8, 128), 0)
    lane = lax.broadcasted_iota(jnp.int32, (8, 128), 1)
    tiles = NORB // 8
    st = [matrix[8 * t : 8 * t + 8, :] for t in range(tiles)]
    et = [jnp.where(lane == sub + 8 * t, 1.0, 0.0).astype(F32) for t in range(tiles)]
    for j in range(0, NORB, wide):
        t0, r = divmod(j, 8)
        cols = [[over_lanes(st[t], j + k) for k in range(wide)] for t in range(t0, tiles)]
        a = {(k, q): over_rows(cols[0][q], r + k) for k in range(wide) for q in range(k + 1)}
        inv, low = [], {}
        for p in range(wide):
            inv.append(1.0 / a[p, p])
            for k in range(p + 1, wide):
                low[k, p] = a[k, p] * inv[p]
            for k in range(p + 1, wide):
                for q in range(p + 1, k + 1):
                    a[k, q] = a[k, q] - low[k, p] * a[q, p]

        def forward(rows):
            done = []
            for k, row in enumerate(rows):
                for p in range(k):
                    row = row - low[k, p] * done[p]
                done.append(row)
            return done

        srow = forward([over_rows(st[t0], r + k) for k in range(wide)])
        erow = forward([over_rows(et[t0], r + k) for k in range(wide)])
        sdiv = [row * i for row, i in zip(srow, inv)]
        ediv = [row * i for row, i in zip(erow, inv)]
        for t in range(t0, tiles):
            if t == t0 and r + wide == 8:
                continue
            mult = []
            for k in range(wide):
                col = cols[t - t0][k]
                for p in range(k):
                    col = col - mult[p] * low[k, p]
                mult.append(col)
            if t == t0:
                mult = [jnp.where(sub >= r + wide, col, 0.0) for col in mult]
            for k in range(wide):
                st[t] = st[t] - mult[k] * sdiv[k]
                et[t] = et[t] - mult[k] * ediv[k]
        for k in range(wide):
            et[t0] = jnp.where(sub == r + k, erow[k] * lax.rsqrt(a[k, k]), et[t0])
    return jnp.concatenate(et, axis=0)


def kernel(
    orb_ref, pot_ref, out_ref, sub_ref,
    buf0, buf1, potb, w, scal, every, gram, r1, r2, mine, full, rot, inv, sub,
    in_send, in_recv, p_send, p_recv, g_send, g_recv, h_send, h_recv, m_send, m_recv, mates,
    r1_send, r1_recv, r2_send, r2_recv, r3_send, full_recv, o_send, o_recv, sub_sem,
):
    d, o = lax.axis_index("dom"), lax.axis_index("orb")
    y_lo, z, c = d // 32, (d // 2) % 16, d % 2
    prow, pcol = d // 8, d % 8
    off = jnp.maximum(z - y_lo, 0)
    slot = (off * 3 + 2) // 8
    active = (z >= y_lo) & (slot < 6) & ((slot * 8) // 3 == off)
    orbital = slot * 2 + y_lo
    selfpair = active & (c == y_lo)
    meet_row = (o + 16 - z) % 8
    meets = meet_row < 6
    tile = y_lo * 8 + o
    owns = tile < 12

    def far_pencil(i):
        return (2 * z + 17 + jnp.where(i % 2 == 0, 32 - i // 2, (i + 1) // 2)) % 32

    def far_group(i):
        across = (i < 3) | (i == 4)
        along = jnp.where((i == 0) | (i == 3), 2, jnp.where((i == 1) | (i == 5), 1, jnp.where((i == 2) | (i == 6), 3, 0)))
        return ((o // 4 + across.astype(jnp.int32)) % 2) * 4 + (o % 4 + along) % 4

    barrier = pltpu.get_barrier_semaphore()

    def greet(cond, axes):
        @when(cond)
        def _():
            pl.semaphore_signal(barrier, inc=1, device_id=axes, device_id_type=MESH)

    def start(here, src, dst, send, recv, axes):
        @when(here)
        def _():
            pltpu.make_async_copy(src, dst, recv).start()

        @when(jnp.logical_not(here))
        def _():
            copy_to(src, dst, send, recv, axes).start()

    def left(here, src, dst, send, recv, axes):
        @when(jnp.logical_not(here))
        def _():
            copy_to(src, dst, send, recv, axes).wait_send()

    @when(active)
    def _():
        def source(i):
            m = c * 32 + far_pencil(i)
            greet(m != d, {"dom": m})

        loop(32, source)

    loop(8, lambda b: greet(b != o, {"orb": b}))

    partner = {"dom": d + 1 - 2 * c}

    @when(active)
    def _():
        margin, side = jnp.zeros((EXT_COLS, 128), F32), jnp.zeros((8, 128), F32)

        def clear(i):
            buf1[i] = margin
            buf0[i, 0:8, :] = side
            buf0[i, 72:80, :] = side

        loop(EXT_ROWS, clear)

        def clear_rows(i):
            buf0[i] = margin
            buf0[i + EXT_ROWS - RADIUS] = margin

        loop(RADIUS, clear_rows)
        gap = jnp.abs(
            lax.broadcasted_iota(jnp.int32, (128, 128), 0) - lax.broadcasted_iota(jnp.int32, (128, 128), 1)
        )
        weights = jnp.zeros((128, 128), F32)
        for k in range(1, RADIUS + 1):
            weights = jnp.where(gap == k, -0.5 * COEF[k], weights)
        high = weights.astype(jnp.bfloat16)
        rest = weights - high.astype(F32)
        middle = rest.astype(jnp.bfloat16)
        low = (rest - middle.astype(F32)).astype(jnp.bfloat16)
        for i, row in enumerate(((high, middle, high), (high, middle, low))):
            for n, part in enumerate(row):
                w[128 * i : 128 * i + 128, 128 * n : 128 * n + 128] = part
        for s, row in enumerate(step_scalars()):
            for i, value in enumerate(row):
                scal[3 * s + i] = jnp.float32(value)
        greet(active, partner)

    pl.semaphore_wait(barrier, 19 + active.astype(jnp.int32) - selfpair.astype(jnp.int32))

    far = (((z + 8) % 16) * 3) // 4
    col0 = pl.multiple_of(pcol * 8, 8)

    def far_first(i):
        return (far + 12 + jnp.where(i % 2 == 0, -(i // 2), (i + 1) // 2)) % 12

    def pot_args(j):
        t = holder(j, y_lo)
        return t == d, pot_ref.at[0, o], potb.at[prow % 4, o, pl.ds(col0, 8)], p_send.at[j], p_recv.at[prow % 4], {"dom": t}

    def in_args(j):
        t = holder(j, y_lo)
        dst = buf0.at[pl.ds(RADIUS + (prow % 4) * 6, 6), pl.ds(pl.multiple_of(8 + pcol * 8, 8), 8)]
        return t == d, orb_ref.at[j, 0], dst, in_send.at[j], in_recv, {"dom": t}

    @when(o < 6)
    def _():
        loop(12, lambda i: start(*pot_args(far_first(i))))

    def send_in(first, count):
        loop(count, lambda i: start(*in_args(far_first(first + i))))

    @when(jnp.logical_not(active))
    def _():
        send_in(0, 12)


    def share_args(n):
        q, b = n // 8, n % 8
        return b == o, potb.at[q, o], potb.at[q, o], g_send.at[n], g_recv.at[o], {"orb": b}

    def out_args(what, m, r):
        src = (buf0, buf1)[what].at[RADIUS + (m // 8) * 6 + r, pl.ds(pl.multiple_of(8 + (m % 8) * 8, 8), 8)]
        t = c * 32 + m
        b = (r + m // 2) % 8
        axes = {"orb": b, "dom": t}
        return (t == d) & (b == o), src, every.at[what, o * 12 + orbital], m_send.at[what, m], m_recv.at[what], axes

    def gone(what, first, count):
        def one(i):
            m = far_pencil(first + i)
            alone = (c * 32 + m == d) & meets

            @when(alone)
            def _():
                landed(every.at[what, pl.ds(0, 5)], m_send.at[what, m])

            @when(jnp.logical_not(alone))
            def _():
                landed(every.at[what, pl.ds(0, 6)], m_send.at[what, m])

        loop(count, one)

    @when(active)
    def _():
        def share(first, count):
            def part(n):
                i = first + n
                q = (z // 4 + jnp.where(i == 2, 3, jnp.where(i == 3, 2, i))) % 4
                landed(potb.at[q, 0], p_recv.at[q])

                def one(b):
                    here, src, dst, send, recv, axes = share_args(q * 8 + far_group(b))

                    @when(jnp.logical_not(here))
                    def _():
                        copy_to(src, dst, send, recv, axes).start()

                loop(8, one)

            @when(o < 6)
            def _():
                loop(count, part)

        share(0, 2)
        send_in(0, 4)
        share(2, 1)
        send_in(4, 4)
        share(3, 1)
        send_in(8, 4)

        def shared(r):
            @when(r != o)
            def _():
                landed(potb.at[:, 0], g_recv.at[r])

        loop(6, shared)
        landed(buf0.at[pl.ds(RADIUS, ROWS), pl.ds(8, 64)], in_recv)

        def tell(b):
            @when(b != o)
            def _():
                pl.semaphore_signal(mates, inc=1, device_id={"orb": b}, device_id_type=MESH)

        loop(8, tell)

        def step(s, what, cur, new):
            halo = copy_to(
                cur.at[pl.ds(24 - 18 * c, 6), pl.ds(8, 64)],
                cur.at[pl.ds(30 * c, 6), pl.ds(8, 64)],
                h_send.at[what], h_recv.at[what], partner,
            )
            halo.start()
            scale, shift, past = scal[3 * s], scal[3 * s + 1], scal[3 * s + 2]
            x = cur[RADIUS : RADIUS + ROWS, 8:72, :].reshape(ROWS * 64, 128)
            high = x.astype(jnp.bfloat16)
            rest = x - high.astype(F32)
            middle = rest.astype(jnp.bfloat16)
            low = (rest - middle.astype(F32)).astype(jnp.bfloat16)
            most = jnp.dot(jnp.concatenate([high, middle], axis=1), w[:, :256], preferred_element_type=F32)
            small = jnp.dot(jnp.concatenate([low, high], axis=1), w[:, 256:], preferred_element_type=F32)
            along = ((most[:, 128:] + small) + most[:, :128]).reshape(ROWS, 64, 128)
            new[RADIUS : RADIUS + ROWS, 8:72, :] = scale * along - past * new[RADIUS : RADIUS + ROWS, 8:72, :]

            def block(i):
                @when(i == 3)
                def _():
                    halo.wait_recv()

                blk = jnp.where(c == 0, i, 3 - i)
                r0 = RADIUS + blk * 6
                for yt in range(8):
                    y0 = 8 + 8 * yt
                    col = [cur[r0 - RADIUS + m, y0 : y0 + 8, :] for m in range(18)]
                    for i6 in range(6):
                        r = r0 + i6
                        mid = col[i6 + RADIUS]
                        acc = (potb[blk, i6, y0 - 8 : y0, :] - shift) * mid
                        for k in range(1, RADIUS + 1):
                            term = col[i6 + RADIUS + k] + col[i6 + RADIUS - k]
                            term = term + (cur[r, y0 + k : y0 + k + 8, :] + cur[r, y0 - k : y0 - k + 8, :])
                            acc = acc + (-0.5 * COEF[k]) * term
                        new[r, y0 : y0 + 8, :] = scale * acc + new[r, y0 : y0 + 8, :]

            loop(4, block)
            halo.wait_send()

        def two_steps(i):
            step(2 * i + 1, 0, buf0, buf1)

            @when(i < 4)
            def _():
                step(2 * i + 2, 1, buf1, buf0)

            @when(i == 3)
            def _():
                pl.semaphore_wait(mates, 7)
                loop(192, lambda n: start(*out_args(0, far_pencil(n // 6), n % 6)))

        loop(5, two_steps)
        gone(0, 0, 28)
        loop(192, lambda n: start(*out_args(1, far_pencil(n // 6), n % 6)))

    def r1_args(what, m):
        axes = {"orb": m % 8, "dom": (m // 8) * 32 + z * 2 + what}
        here = (tile == m) & (c == what)
        return here, gram.at[what, m], r1.at[meet_row * 4 + y_lo * 2 + c], r1_send.at[what, m], r1_recv, axes

    def r2_args(b):
        return b == z, mine.at[0], r2.at[z], r2_send.at[b], r2_recv, {"dom": y_lo * 32 + b * 2 + c}

    def r3_args(n):
        b, y, core = n // 4, (n // 2) % 2, n % 2
        here = (b == o) & (y == y_lo) & (core == c)
        axes = {"orb": b, "dom": y * 32 + z * 2 + core}
        return here, mine.at[1], full.at[c, tile], r3_send.at[n], full_recv.at[c], axes

    def meet_sums(what):
        @when(meets)
        def _():
            landed(every.at[what], m_recv.at[what])
            left_parts, right_parts = split(every, 0), split(every, what)
            pairs = ((0, 0), (0, 1), (1, 0), (1, 1), (0, 2), (2, 0))
            acc = lax.dot_general(
                jnp.concatenate([left_parts[a] for a, _ in pairs], axis=1),
                jnp.concatenate([right_parts[b] for _, b in pairs], axis=1),
                (((1,), (1,)), ((), ())), preferred_element_type=F32,
            )
            for m in range(12):
                gram[what, m] = jnp.zeros((8, 128), F32)
                gram[what, m, :, 0:NORB] = acc[8 * m : 8 * m + 8, :]
            loop(12, lambda m: start(*r1_args(what, m)))

    def plane_sum(what):
        @when(owns & (c == what))
        def _():
            landed(r1, r1_recv)
            parts = [r1[b] for b in range(24)]
            while len(parts) > 1:
                parts = [sum(parts[i + 1 : i + 2], parts[i]) for i in range(0, len(parts), 2)]
            mine[0] = parts[0]
            loop(16, lambda i: start(*r2_args((z + 8 + jnp.where(i % 2 == 0, 16 - i // 2, (i + 1) // 2)) % 16)))

    def whole_sum(what):
        @when(owns & (c == what))
        def _():
            landed(r2, r2_recv)
            parts = [r2[b] for b in range(16)]
            while len(parts) > 1:
                parts = [parts[i] + parts[i + 1] for i in range(0, len(parts), 2)]
            mine[1] = parts[0] * (1.0 / CELLS)
            loop(32, lambda n: start(*r3_args(far_group(n // 4) * 4 + n % 4)))

    meet_sums(0)
    plane_sum(0)
    meet_sums(1)
    whole_sum(0)
    plane_sum(1)
    landed(full.at[0], full_recv.at[0])
    inverse = inverse_factor(full[0].reshape(NORB, 128))[:, :NORB]

    def o_args(b):
        dst = out_ref.at[:, 0, meet_row]
        return b == o, rot.at[pl.ds(b * 12, 12)], dst, o_send.at[b], o_recv, {"orb": b}

    @when(meets)
    def _():
        inv[...] = inverse

        def rotate(i):
            half = (o // 4 + 1 + i) % 2
            rows = pl.ds(pl.multiple_of(half * 48, 8), 48)
            part = inv[rows, :]
            for s in range(8):
                rot[rows, s, :] = jnp.dot(part, every[0, :, s, :], precision=HI, preferred_element_type=F32)
            loop(4, lambda n: start(*o_args(half * 4 + (o % 4 + jnp.where(n == 0, 2, n + n // 3 - 1)) % 4)))

        loop(2, rotate)

    whole_sum(1)

    loop(12, lambda j: left(*in_args(j)))

    @when(o < 6)
    def _():
        loop(12, lambda j: left(*pot_args(j)))

    @when(active)
    def _():
        @when(o < 6)
        def _():
            loop(32, lambda n: left(*share_args(n)))

        gone(0, 28, 4)
        gone(1, 0, 32)

    for what in range(2):

        @when(meets)
        def _():
            loop(12, lambda m: left(*r1_args(what, m)))

    landed(full.at[1], full_recv.at[1])
    projected = full[1].reshape(NORB, 128)[:, :NORB]
    half = jnp.dot(inverse, projected, precision=HI, preferred_element_type=F32)
    sub[...] = lax.dot_general(
        half, inverse, (((1,), (1,)), ((), ())), precision=HI, preferred_element_type=F32
    )
    give = pltpu.make_async_copy(sub, sub_ref, sub_sem)
    give.start()

    @when(owns)
    def _():
        loop(16, lambda b: left(*r2_args(b)))
        loop(32, lambda n: left(*r3_args(n)))

    @when(meets)
    def _():
        loop(8, lambda b: left(*o_args(b)))

    landed(out_ref, o_recv)
    give.wait()


def local(orbitals, potential):
    anyspace = pl.BlockSpec(memory_space=pl.ANY)
    dma = pltpu.SemaphoreType.DMA
    return pl.pallas_call(
        kernel,
        out_shape=(
            jax.ShapeDtypeStruct(orbitals.shape, F32),
            jax.ShapeDtypeStruct((NORB, NORB), F32),
        ),
        in_specs=[anyspace, anyspace],
        out_specs=(anyspace, anyspace),
        scratch_shapes=[
            pltpu.VMEM((EXT_ROWS, EXT_COLS, 128), F32),
            pltpu.VMEM((EXT_ROWS, EXT_COLS, 128), F32),
            pltpu.VMEM((4, 6, 64, 128), F32),
            pltpu.VMEM((256, 384), jnp.bfloat16),
            pltpu.SMEM((32,), F32),
            pltpu.VMEM((2, NORB, 8, 128), F32),
            pltpu.VMEM((2, 12, 8, 128), F32),
            pltpu.VMEM((24, 8, 128), F32),
            pltpu.VMEM((16, 8, 128), F32),
            pltpu.VMEM((2, 8, 128), F32),
            pltpu.VMEM((2, 12, 8, 128), F32),
            pltpu.VMEM((NORB, 8, 128), F32),
            pltpu.VMEM((NORB, NORB), F32),
            pltpu.VMEM((NORB, NORB), F32),
            dma((12,)), dma, dma((12,)), dma((4,)), dma((32,)), dma((6,)), dma((2,)), dma((2,)),
            dma((2, 32)), dma((2,)), pltpu.SemaphoreType.REGULAR,
            dma((2, 12)), dma, dma((16,)), dma, dma((32,)), dma((2,)), dma((8,)), dma, dma,
        ],
        compiler_params=pltpu.CompilerParams(
            collective_id=0, has_side_effects=True, vmem_limit_bytes=60 * 2**20
        ),
        name="filter_and_rotate",
    )(orbitals, potential)


def solution(mesh):
    return jax.shard_map(
        local,
        mesh=mesh,
        in_specs=(P("orb", "dom", None, None, None), P("dom", None, None, None)),
        out_specs=(P("orb", "dom", None, None, None), P()),
        check_vma=False,
    )
```
